32 devices in a mesh: groups: 2 (over x), rows: 8 (over z, y), pairs: 2 (over core).
Axes of the slice: x: 2, y: 2, z: 4, core: 2. Of those that a mesh axis runs over, the one named last changes fastest.
Arguments:
- matrix: float32 [4096, 2048], P(('groups', 'rows'), 'pairs'), parts along dimension 0, may hold values from -150 to 150
- plan: int32 [1, 16], replicated, may hold values from 0 to 15, as said below
Outputs:
- rotated: float32 [4096, 2048], P(('groups', 'rows'), 'pairs'), parts along dimension 0
The draws below stay inside these ranges and needn't reach their ends.
There are 2 independent parts, one for each index of `groups`. The reference program is written for one: setup_inputs(seed, part) draws one part's arguments, and reference() takes and returns one part's arrays. A program takes and returns all parts, laid end to end along the dimension named above; an argument that names none is the same for every part. Nothing has to cross between parts.
Inputs may be any that keep to these rules, and one draw needn't show every extreme that they name: `plan`: each row is a permutation of the 16 blocks; positions 2s and 2s + 1 of a row form a pair, and the rows are consecutive rounds of one round-robin tournament, so no pair repeats.
All inputs are finite; a program needn't handle non-finite values.
Results may differ from the reference program's by a relative error of at most 0.0003.
Values sent between devices are 32-bit elements; how exact they have to be, the bound alone decides.
No kernel may reach another device: no remote copies, remote signals or barrier semaphores. Data moves between devices by JAX's collectives and lax.ppermute only.
A program may use at most 64 MiB of HBM per device.

```python
import jax
import jax.numpy as jnp
from jax import lax

BW = 128
ROUNDS = 1
STEPS = 4
ROWS = 2048
NB = 16
N = 2048


def draw_matrix(key, part):
    key = jax.random.fold_in(key, 11)
    keys = jax.random.split(key, 4)
    col_scale = jnp.exp(jax.random.uniform(keys[0], (1, N), jnp.float32, jnp.log(0.3), jnp.log(3.0)))
    noise = jax.random.normal(keys[1], (ROWS, N), jnp.float32)
    strength = 0.6
    common = jax.random.normal(keys[2], (ROWS, 1), jnp.float32)
    loading = jax.random.normal(keys[3], (1, N), jnp.float32) * strength
    return ((noise + common * loading) * col_scale).astype(jnp.float32)


def draw_plan(key, part):
    key = jax.random.fold_in(key, 23)
    first_key, second_key = jax.random.split(key)
    relabel = jax.random.permutation(first_key, NB).astype(jnp.int32)
    start = jax.random.randint(second_key, (), 0, NB - 1)
    slot = jnp.arange(NB // 2, dtype=jnp.int32)[None, :]
    turn = (start + jnp.arange(ROUNDS, dtype=jnp.int32)[:, None]) % (NB - 1)
    first = jnp.where(slot == 0, NB - 1, (turn + slot) % (NB - 1))
    second = (turn - slot) % (NB - 1)
    players = jnp.stack([first, second], axis=2).reshape(ROUNDS, NB)
    return relabel[players].astype(jnp.int32)


def setup_inputs(seed: int = 0, part: int = 0) -> dict:
    splits = jax.random.split(jax.random.key(seed), 3)
    part_splits = jax.random.split(jax.random.fold_in(splits[2], part), 3)
    return {
        "matrix": draw_matrix(jax.random.fold_in(jax.random.fold_in(splits[2], part), 71), part),
        "plan": draw_plan(jax.random.fold_in(splits[2], 71), part),
    }


def turn_pairs(values, cos_part, sin_part, shift, axis):
    half = values.shape[axis] // 2
    upper = lax.slice_in_dim(values, 0, half, axis=axis)
    lower = jnp.roll(lax.slice_in_dim(values, half, 2 * half, axis=axis), -shift, axis=axis)
    new_upper = cos_part * upper - sin_part * lower
    new_lower = sin_part * upper + cos_part * lower
    return jnp.concatenate([new_upper, jnp.roll(new_lower, shift, axis=axis)], axis=axis)


def jacobi(gram_full):
    count, order, _ = gram_full.shape
    half = order // 2
    basis = jnp.broadcast_to(jnp.eye(order, dtype=gram_full.dtype), gram_full.shape)
    for step in range(STEPS):
        shift = step % half
        diag_all = jnp.diagonal(gram_full, axis1=1, axis2=2)
        diag_upper = diag_all[:, :half]
        diag_lower = jnp.roll(diag_all[:, half:], -shift, axis=1)
        cross = jnp.diagonal(jnp.roll(gram_full[:, :half, half:], -shift, axis=2), axis1=1, axis2=2)
        spread = diag_lower - diag_upper
        orient = jnp.where(spread >= 0, 1.0, -1.0).astype(gram_full.dtype)
        angle = 0.5 * jnp.arctan2(2.0 * cross * orient, spread * orient)
        cos_v = jnp.cos(angle)
        sin_v = jnp.sin(angle)
        gram_full = turn_pairs(gram_full, cos_v[:, :, None], sin_v[:, :, None], shift, 1)
        gram_full = turn_pairs(gram_full, cos_v[:, None, :], sin_v[:, None, :], shift, 2)
        basis = turn_pairs(basis, cos_v[:, None, :], sin_v[:, None, :], shift, 2)
    return basis


def reference(matrix, plan):
    total_rows = matrix.shape[0]
    blocks = matrix.reshape(total_rows, NB, BW)
    for round_index in range(ROUNDS):
        order = plan[round_index].astype(jnp.int32)
        picked = jnp.take(blocks, order, axis=1)
        paired = picked.reshape(total_rows, NB // 2, 2 * BW)
        gram_full = jnp.einsum("rpi,rpj->pij", paired, paired, precision=lax.Precision.HIGHEST)
        basis = jacobi(gram_full)
        turned = jnp.einsum("rpi,pij->rpj", paired, basis, precision=lax.Precision.HIGHEST)
        blocks = blocks.at[:, order, :].set(turned.reshape(total_rows, NB, BW))
    return blocks.reshape(total_rows, NB * BW)
```

```python
import jax
import jax.numpy as jnp
from jax import lax
from jax.experimental import pallas as pl
from jax.experimental.pallas import tpu as pltpu
from jax.sharding import PartitionSpec as P

BW = 128
STEPS = 4
SUB = 8
BANDS = [(kind, d) for d in range(STEPS) for kind in ("uu", "ll", "ul", "lu") if (kind, d) != ("lu", 0)]


def ahead(values, d):
    return values if d == 0 else pltpu.roll(values, BW - d, 1)


def start_fetch(order, mine, other, buf, sem):
    held = mine.shape[1] // BW
    me = lax.axis_index("pairs")

    def fetch(i, carry):
        block = order[0, i]
        columns = pl.ds(pl.multiple_of((block % held) * BW, BW), BW)

        @pl.when(block // held == me)
        def _():
            pltpu.make_async_copy(mine.at[:, columns], buf.at[i], sem.at[i]).start()

        @pl.when(block // held != me)
        def _():
            pltpu.make_async_copy(other.at[:, columns], buf.at[i], sem.at[i]).start()

        return carry

    lax.fori_loop(0, order.shape[1], fetch, 0)


def await_fetch(mine, buf, sem, i):
    pltpu.make_async_copy(mine.at[:, pl.ds(0, BW)], buf.at[i], sem.at[i]).wait()


def band_kernel(order, mine, other, bands, buf, sem):
    start_fetch(order, mine, other, buf, sem)
    rows = mine.shape[0]

    def one_pair(pair, carry):
        await_fetch(mine, buf, sem, 2 * pair)
        await_fetch(mine, buf, sem, 2 * pair + 1)
        sums = [None] * len(BANDS)
        for row in range(0, rows, SUB):
            u = buf[2 * pair, pl.ds(row, SUB), :]
            l = buf[2 * pair + 1, pl.ds(row, SUB), :]
            us = [ahead(u, d) for d in range(STEPS)]
            ls = [ahead(l, d) for d in range(STEPS)]
            for n, (kind, d) in enumerate(BANDS):
                term = (u if kind[0] == "u" else l) * (us if kind[1] == "u" else ls)[d]
                sums[n] = term if sums[n] is None else sums[n] + term
        for n in range(len(BANDS)):
            bands[n, pl.ds(pair, 1), :] = jnp.sum(sums[n], axis=0, keepdims=True)
        return carry

    lax.fori_loop(0, order.shape[1] // 2, one_pair, 0)


def rotation(upper, lower, cross):
    spread = lower - upper
    twice = jnp.where(spread >= 0, 2.0 * cross, -2.0 * cross)
    spread = jnp.abs(spread)
    scale = jnp.maximum(spread, jnp.abs(twice))
    zero = scale == 0
    scale = jnp.where(zero, 1.0, scale)
    x = jnp.where(zero, 1.0, spread / scale)
    y = twice / scale
    length = jnp.sqrt(x * x + y * y)
    cos_v = jnp.sqrt(0.5 + 0.5 * (x / length))
    sin_v = y / (2.0 * length * cos_v)
    return cos_v, sin_v


def jacobi_bands(g):
    turns = []
    for step in range(STEPS):
        cos_v, sin_v = rotation(g["uu", 0], g["ll", 0], g["ul", 0])
        turns.append((cos_v, sin_v))
        left = STEPS - 1 - step
        if left == 0:
            break
        new = {}
        for d in range(left + 1):
            cos_d, sin_d = ahead(cos_v, d), ahead(sin_v, d)
            uu, ll, ul = g["uu", d], g["ll", d], g["ul", d]
            lu = g["lu", d] if d else ul
            a, b = cos_v * uu - sin_v * lu, cos_v * ul - sin_v * ll
            e, f = sin_v * uu + cos_v * lu, sin_v * ul + cos_v * ll
            new["uu", d] = cos_d * a - sin_d * b
            new["ul", d] = sin_d * a + cos_d * b
            new["lu", d] = cos_d * e - sin_d * f
            new["ll", d] = sin_d * e + cos_d * f
        g = {}
        for d in range(left):
            g["uu", d] = new["uu", d]
            g["ll", d] = ahead(new["ll", d], 1)
            g["ul", d] = new["ul", d + 1]
            if d:
                g["lu", d] = ahead(new["ul", 0] if d == 1 else new["lu", d - 1], 1)
    return turns


def turn_kernel(order, bands, mine, other, out, buf, turned, cs, sem, out_sem):
    start_fetch(order, mine, other, buf, sem)
    rows = mine.shape[0]
    held = mine.shape[1] // BW
    me = lax.axis_index("pairs")
    for step, (cos_v, sin_v) in enumerate(jacobi_bands({key: bands[n] for n, key in enumerate(BANDS)})):
        cs[2 * step] = cos_v
        cs[2 * step + 1] = sin_v

    def write_back(i):
        block = order[0, i]

        @pl.when(block // held == me)
        def _():
            slot = block % held
            columns = pl.ds(pl.multiple_of(slot * BW, BW), BW)
            pltpu.make_async_copy(turned.at[i], out.at[:, columns], out_sem.at[slot]).start()

    def one_pair(pair, carry):
        first, second = 2 * pair, 2 * pair + 1
        await_fetch(mine, buf, sem, first)
        await_fetch(mine, buf, sem, second)

        @pl.when((order[0, first] // held == me) | (order[0, second] // held == me))
        def _():
            turns = [
                jnp.broadcast_to(cs[n, pl.ds(pair, 1), :], (SUB, BW)) for n in range(2 * STEPS)
            ]
            for row in range(0, rows, SUB):
                u = buf[first, pl.ds(row, SUB), :]
                l = buf[second, pl.ds(row, SUB), :]
                for step in range(STEPS):
                    cos_v, sin_v = turns[2 * step], turns[2 * step + 1]
                    u, l = cos_v * u - sin_v * l, sin_v * u + cos_v * l
                    l = ahead(l, 1) if step < STEPS - 1 else ahead(l, BW - (STEPS - 1))
                turned[first, pl.ds(row, SUB), :] = u
                turned[second, pl.ds(row, SUB), :] = l

        write_back(first)
        write_back(second)
        return carry

    lax.fori_loop(0, order.shape[1] // 2, one_pair, 0)
    for slot in range(held):
        pltpu.make_async_copy(turned.at[slot], out.at[:, pl.ds(slot * BW, BW)], out_sem.at[slot]).wait()


def sum_over_rows(values):
    size = lax.axis_size("rows")
    if size & (size - 1):
        return lax.psum(values, "rows")
    stride = 1
    while stride < size:
        values = values + lax.ppermute(values, "rows", [(i, i ^ stride) for i in range(size)])
        stride *= 2
    return values


def body(matrix, plan):
    rows, width = matrix.shape
    count = width // BW * lax.axis_size("pairs")
    other = lax.ppermute(matrix, "pairs", [(0, 1), (1, 0)])
    smem = pl.BlockSpec(memory_space=pltpu.SMEM)
    vmem = pl.BlockSpec(memory_space=pltpu.VMEM)
    hbm = pl.BlockSpec(memory_space=pl.ANY)
    blocks = pltpu.VMEM((count, rows, BW), jnp.float32)
    params = pltpu.CompilerParams(vmem_limit_bytes=16 * 1024 * 1024)
    bands = pl.pallas_call(
        band_kernel,
        out_shape=jax.ShapeDtypeStruct((len(BANDS), count // 2, BW), jnp.float32),
        in_specs=[smem, hbm, hbm],
        out_specs=vmem,
        scratch_shapes=[blocks, pltpu.SemaphoreType.DMA((count,))],
        compiler_params=params,
        name="gram_bands",
    )(plan, matrix, other)
    bands = sum_over_rows(bands)
    return pl.pallas_call(
        turn_kernel,
        out_shape=jax.ShapeDtypeStruct((rows, width), jnp.float32),
        in_specs=[smem, vmem, hbm, hbm],
        out_specs=hbm,
        scratch_shapes=[
            blocks,
            blocks,
            pltpu.VMEM((2 * STEPS, count // 2, BW), jnp.float32),
            pltpu.SemaphoreType.DMA((count,)),
            pltpu.SemaphoreType.DMA((width // BW,)),
        ],
        compiler_params=params,
        name="turn_columns",
    )(plan, bands, matrix, other)


def solution(mesh):
    return jax.shard_map(
        body,
        mesh=mesh,
        in_specs=(P(("groups", "rows"), "pairs"), P()),
        out_specs=P(("groups", "rows"), "pairs"),
        check_vma=False,
    )
```

```python
import functools

import jax
import jax.numpy as jnp
from jax import lax
from jax.experimental import pallas as pl
from jax.experimental.pallas import tpu as pltpu
from jax.sharding import PartitionSpec as P

BW = 128
STEPS = 4
SUB = 8
BANDS = (
    [("uu", d) for d in range(STEPS)]
    + [("ll", d) for d in range(STEPS)]
    + [("ul", d) for d in range(STEPS)]
    + [("lu", d) for d in range(1, STEPS)]
)
CROSS = BANDS[2 * STEPS :]
ROWS_SENT = 16
SMEM = pl.BlockSpec(memory_space=pltpu.SMEM)
VMEM = pl.BlockSpec(memory_space=pltpu.VMEM)
HBM = pl.BlockSpec(memory_space=pl.ANY)
PARAMS = pltpu.CompilerParams(vmem_limit_bytes=16 * 1024 * 1024)


def ahead(values, d):
    return values if d == 0 else pltpu.roll(values, BW - d, 1)


def columns_of(slot):
    return pl.ds(pl.multiple_of(slot * BW, BW), BW)


def self_sums(columns, store):
    sums = [0.0] * STEPS
    for row in range(0, columns.rows, SUB):
        u = columns(row)
        for d in range(STEPS):
            sums[d] = sums[d] + u * ahead(u, d)
    for d in range(STEPS):
        store(d, sums[d])


class Block:
    def __init__(self, ref, slot):
        self.ref, self.columns, self.rows = ref, columns_of(slot), ref.shape[0]

    def __call__(self, row):
        return self.ref[pl.ds(row, SUB), self.columns]


def self_kernel(mine, out):
    def one(slot, carry):
        def store(d, value):
            out[slot, d] = value

        self_sums(Block(mine, slot), store)
        return carry

    lax.fori_loop(0, mine.shape[1] // BW, one, 0)


def gram_kernel(order, own, mine, other, bands, theirs, cross):
    held = mine.shape[1] // BW
    pairs = order.shape[1] // 2
    me = lax.axis_index("pairs")

    def one(slot, carry):
        def store(d, value):
            theirs[slot, d] = value

        self_sums(Block(other, slot), store)
        return carry

    lax.fori_loop(0, held, one, 0)

    def one_pair(pair, carry):
        first, second = order[0, 2 * pair], order[0, 2 * pair + 1]
        first_mine, second_mine = first // held == me, second // held == me

        def go(u_ref, l_ref):
            u_block, l_block = Block(u_ref, first % held), Block(l_ref, second % held)
            sums = [0.0] * len(CROSS)
            for row in range(0, u_block.rows, SUB):
                u, l = u_block(row), l_block(row)
                for n, (kind, d) in enumerate(CROSS):
                    sums[n] = sums[n] + (u * ahead(l, d) if kind == "ul" else l * ahead(u, d))
            for n in range(len(CROSS)):
                cross[pair, n] = sums[n]

        for u_here in (True, False):
            for l_here in (True, False):
                pl.when((first_mine == u_here) & (second_mine == l_here))(
                    functools.partial(go, mine if u_here else other, mine if l_here else other)
                )
        return carry

    lax.fori_loop(0, pairs, one_pair, 0)

    def one_sum(pair, carry):
        for side in range(2):
            block = order[0, 2 * pair + side]

            def go(ref):
                for d in range(STEPS):
                    bands[pair, pl.ds(side * STEPS + d, 1), :] = jnp.sum(
                        ref[block % held, d], axis=0, keepdims=True
                    )

            pl.when(block // held == me)(functools.partial(go, own))
            pl.when(block // held != me)(functools.partial(go, theirs))
        for n in range(len(CROSS)):
            bands[pair, pl.ds(2 * STEPS + n, 1), :] = jnp.sum(cross[pair, n], axis=0, keepdims=True)
        bands[pair, pl.ds(ROWS_SENT - 1, 1), :] = jnp.zeros((1, BW), jnp.float32)
        return carry

    lax.fori_loop(0, pairs, one_sum, 0)


def rotation(upper, lower, cross):
    spread = lower - upper
    twice = jnp.where(spread >= 0, 2.0 * cross, -2.0 * cross)
    spread = jnp.abs(spread)
    scale = jnp.maximum(spread, jnp.abs(twice))
    zero = scale == 0
    scale = jnp.where(zero, 1.0, scale)
    x = jnp.where(zero, 1.0, spread / scale)
    y = twice / scale
    length = jnp.sqrt(x * x + y * y)
    cos_v = jnp.sqrt(0.5 + 0.5 * (x / length))
    sin_v = y / (2.0 * length * cos_v)
    return cos_v, sin_v


def jacobi_bands(g):
    turns = []
    for step in range(STEPS):
        cos_v, sin_v = rotation(g["uu", 0], g["ll", 0], g["ul", 0])
        turns += [cos_v, sin_v]
        left = STEPS - 1 - step
        if left == 0:
            break
        new = {}
        for d in range(left + 1):
            cos_d, sin_d = ahead(cos_v, d), ahead(sin_v, d)
            uu, ll, ul = g["uu", d], g["ll", d], g["ul", d]
            lu = g["lu", d] if d else ul
            a, b = cos_v * uu - sin_v * lu, cos_v * ul - sin_v * ll
            e, f = sin_v * uu + cos_v * lu, sin_v * ul + cos_v * ll
            new["uu", d] = cos_d * a - sin_d * b
            new["ul", d] = sin_d * a + cos_d * b
            new["lu", d] = cos_d * e - sin_d * f
            new["ll", d] = sin_d * e + cos_d * f
        g = {}
        for d in range(left):
            g["uu", d] = new["uu", d]
            g["ll", d] = ahead(new["ll", d], 1)
            g["ul", d] = new["ul", d + 1]
            if d:
                g["lu", d] = ahead(new["ul", 0] if d == 1 else new["lu", d - 1], 1)
    return turns


def jacobi_kernel(parts, out, total):
    total[...] = jnp.sum(parts[...], axis=0)
    rows = {key: jnp.broadcast_to(total[pl.ds(n, 1), :], (SUB, BW)) for n, key in enumerate(BANDS)}
    turns = jacobi_bands(rows)
    sublane = lax.broadcasted_iota(jnp.int32, (SUB, BW), 0)
    packed = turns[0]
    for n in range(1, 2 * STEPS):
        packed = jnp.where(sublane == n, turns[n], packed)
    for place in range(out.shape[0]):
        out[place] = packed


def turn_kernel(order, turns_ref, mine, other, out, turned, sem):
    held = mine.shape[1] // BW
    pairs = order.shape[1] // 2
    me = lax.axis_index("pairs")

    def send(slot):
        return pltpu.make_async_copy(turned.at[slot], out.at[:, columns_of(slot)], sem.at[slot])

    def one_pair(pair, carry):
        first, second = order[0, 2 * pair], order[0, 2 * pair + 1]
        first_mine, second_mine = first // held == me, second // held == me

        def go(u_here, l_here):
            u_slot, l_slot = first % held, second % held
            u_block = Block(mine if u_here else other, u_slot)
            l_block = Block(mine if l_here else other, l_slot)
            turns = [
                jnp.broadcast_to(turns_ref[pair, pl.ds(n, 1), :], (SUB, BW)) for n in range(2 * STEPS)
            ]
            for row in range(0, u_block.rows, SUB):
                u, l = u_block(row), l_block(row)
                for step in range(STEPS):
                    cos_v, sin_v = turns[2 * step], turns[2 * step + 1]
                    u, l = cos_v * u - sin_v * l, sin_v * u + cos_v * l
                    l = ahead(l, 1 if step < STEPS - 1 else BW - (STEPS - 1))
                if u_here:
                    turned[u_slot, pl.ds(row, SUB), :] = u
                if l_here:
                    turned[l_slot, pl.ds(row, SUB), :] = l
            if u_here:
                send(u_slot).start()
            if l_here:
                send(l_slot).start()

        for u_here, l_here in ((True, True), (True, False), (False, True)):
            pl.when((first_mine == u_here) & (second_mine == l_here))(
                functools.partial(go, u_here, l_here)
            )
        return carry

    lax.fori_loop(0, pairs, one_pair, 0)
    for slot in range(held):
        send(slot).wait()


def spread(values, count):
    size = lax.axis_size("rows")
    groups = None
    if size != count:
        groups = [[base + i for i in range(count)] for base in range(0, size, count)]
    return lax.all_to_all(values, "rows", 0, 0, axis_index_groups=groups, tiled=True)


def sum_pairs(bands):
    pairs = bands.shape[0]
    size = lax.axis_size("rows")
    parts = spread(bands, pairs)
    if size != pairs:
        parts = jnp.sum(parts, axis=0, keepdims=True)
        groups = [list(range(i, size, pairs)) for i in range(pairs)]
        parts = lax.psum(parts, "rows", axis_index_groups=groups)
    return parts


def body(matrix, plan):
    rows, width = matrix.shape
    held = width // BW
    pairs = held * lax.axis_size("pairs") // 2
    other = lax.ppermute(matrix, "pairs", [(0, 1), (1, 0)])
    flops = rows * width * STEPS * 3
    own = pl.pallas_call(
        self_kernel,
        out_shape=jax.ShapeDtypeStruct((held, STEPS, SUB, BW), jnp.float32),
        in_specs=[VMEM],
        out_specs=VMEM,
        compiler_params=PARAMS,
        cost_estimate=pl.CostEstimate(flops=flops, bytes_accessed=4 * rows * width, transcendentals=0),
        name="self_bands",
    )(matrix)
    bands = pl.pallas_call(
        gram_kernel,
        out_shape=jax.ShapeDtypeStruct((pairs, ROWS_SENT, BW), jnp.float32),
        in_specs=[SMEM, VMEM, VMEM, VMEM],
        out_specs=VMEM,
        scratch_shapes=[
            pltpu.VMEM((held, STEPS, SUB, BW), jnp.float32),
            pltpu.VMEM((pairs, len(CROSS), SUB, BW), jnp.float32),
        ],
        compiler_params=PARAMS,
        name="pair_bands",
    )(plan, own, matrix, other)
    parts = sum_pairs(bands)
    turns = pl.pallas_call(
        jacobi_kernel,
        out_shape=jax.ShapeDtypeStruct((pairs, SUB, BW), jnp.float32),
        in_specs=[VMEM],
        out_specs=VMEM,
        scratch_shapes=[pltpu.VMEM((ROWS_SENT, BW), jnp.float32)],
        compiler_params=PARAMS,
        name="jacobi",
    )(parts)
    turns = spread(turns, pairs)
    return pl.pallas_call(
        turn_kernel,
        out_shape=jax.ShapeDtypeStruct((rows, width), jnp.float32),
        in_specs=[SMEM, VMEM, VMEM, VMEM],
        out_specs=HBM,
        scratch_shapes=[
            pltpu.VMEM((held, rows, BW), jnp.float32),
            pltpu.SemaphoreType.DMA((held,)),
        ],
        compiler_params=PARAMS,
        name="turn_columns",
    )(plan, turns, matrix, other)


def solution(mesh):
    return jax.shard_map(
        body,
        mesh=mesh,
        in_specs=(P(("groups", "rows"), "pairs"), P()),
        out_specs=P(("groups", "rows"), "pairs"),
        check_vma=False,
    )
```

```python
import jax
import jax.numpy as jnp
from jax import lax
from jax.experimental import pallas as pl
from jax.experimental.pallas import tpu as pltpu
from jax.sharding import PartitionSpec as P

BW = 128
STEPS = 4
SUB = 8
BANDS = [(kind, d) for d in range(STEPS) for kind in ("uu", "ll", "ul", "lu") if (kind, d) != ("lu", 0)]


def ahead(values, d):
    return values if d == 0 else pltpu.roll(values, BW - d, 1)


def start_fetch(order, mine, other, buf, sem):
    held = mine.shape[1] // BW
    me = lax.axis_index("pairs")

    def fetch(i, carry):
        block = order[0, i]
        columns = pl.ds(pl.multiple_of((block % held) * BW, BW), BW)

        @pl.when(block // held == me)
        def _():
            pltpu.make_async_copy(mine.at[:, columns], buf.at[i], sem.at[i]).start()

        @pl.when(block // held != me)
        def _():
            pltpu.make_async_copy(other.at[:, columns], buf.at[i], sem.at[i]).start()

        return carry

    lax.fori_loop(0, order.shape[1], fetch, 0)


def await_fetch(mine, buf, sem, i):
    pltpu.make_async_copy(mine.at[:, pl.ds(0, BW)], buf.at[i], sem.at[i]).wait()


def band_kernel(order, mine, other, bands, buf, sem):
    start_fetch(order, mine, other, buf, sem)
    rows = mine.shape[0]

    def one_pair(pair, carry):
        await_fetch(mine, buf, sem, 2 * pair)
        await_fetch(mine, buf, sem, 2 * pair + 1)
        sums = [None] * len(BANDS)
        for row in range(0, rows, SUB):
            u = buf[2 * pair, pl.ds(row, SUB), :]
            l = buf[2 * pair + 1, pl.ds(row, SUB), :]
            us = [ahead(u, d) for d in range(STEPS)]
            ls = [ahead(l, d) for d in range(STEPS)]
            for n, (kind, d) in enumerate(BANDS):
                term = (u if kind[0] == "u" else l) * (us if kind[1] == "u" else ls)[d]
                sums[n] = term if sums[n] is None else sums[n] + term
        for n in range(len(BANDS)):
            bands[n, pl.ds(pair, 1), :] = jnp.sum(sums[n], axis=0, keepdims=True)
        return carry

    lax.fori_loop(0, order.shape[1] // 2, one_pair, 0)


def rotation(upper, lower, cross):
    spread = lower - upper
    twice = jnp.where(spread >= 0, 2.0 * cross, -2.0 * cross)
    spread = jnp.abs(spread)
    scale = jnp.maximum(spread, jnp.abs(twice))
    zero = scale == 0
    scale = jnp.where(zero, 1.0, scale)
    x = jnp.where(zero, 1.0, spread / scale)
    y = twice / scale
    length = jnp.sqrt(x * x + y * y)
    cos_v = jnp.sqrt(0.5 + 0.5 * (x / length))
    sin_v = y / (2.0 * length * cos_v)
    return cos_v, sin_v


def jacobi_bands(g):
    turns = []
    for step in range(STEPS):
        cos_v, sin_v = rotation(g["uu", 0], g["ll", 0], g["ul", 0])
        turns.append((cos_v, sin_v))
        left = STEPS - 1 - step
        if left == 0:
            break
        new = {}
        for d in range(left + 1):
            cos_d, sin_d = ahead(cos_v, d), ahead(sin_v, d)
            uu, ll, ul = g["uu", d], g["ll", d], g["ul", d]
            lu = g["lu", d] if d else ul
            a, b = cos_v * uu - sin_v * lu, cos_v * ul - sin_v * ll
            e, f = sin_v * uu + cos_v * lu, sin_v * ul + cos_v * ll
            new["uu", d] = cos_d * a - sin_d * b
            new["ul", d] = sin_d * a + cos_d * b
            new["lu", d] = cos_d * e - sin_d * f
            new["ll", d] = sin_d * e + cos_d * f
        g = {}
        for d in range(left):
            g["uu", d] = new["uu", d]
            g["ll", d] = ahead(new["ll", d], 1)
            g["ul", d] = new["ul", d + 1]
            if d:
                g["lu", d] = ahead(new["ul", 0] if d == 1 else new["lu", d - 1], 1)
    return turns


def turn_kernel(order, bands, mine, other, out, buf, turned, cs, sem, out_sem):
    start_fetch(order, mine, other, buf, sem)
    rows = mine.shape[0]
    held = mine.shape[1] // BW
    me = lax.axis_index("pairs")
    for step, (cos_v, sin_v) in enumerate(jacobi_bands({key: bands[n] for n, key in enumerate(BANDS)})):
        cs[2 * step] = cos_v
        cs[2 * step + 1] = sin_v

    def write_back(i):
        block = order[0, i]

        @pl.when(block // held == me)
        def _():
            slot = block % held
            columns = pl.ds(pl.multiple_of(slot * BW, BW), BW)
            pltpu.make_async_copy(turned.at[i], out.at[:, columns], out_sem.at[slot]).start()

    def one_pair(pair, carry):
        first, second = 2 * pair, 2 * pair + 1
        await_fetch(mine, buf, sem, first)
        await_fetch(mine, buf, sem, second)

        @pl.when((order[0, first] // held == me) | (order[0, second] // held == me))
        def _():
            turns = [
                jnp.broadcast_to(cs[n, pl.ds(pair, 1), :], (SUB, BW)) for n in range(2 * STEPS)
            ]
            for row in range(0, rows, SUB):
                u = buf[first, pl.ds(row, SUB), :]
                l = buf[second, pl.ds(row, SUB), :]
                for step in range(STEPS):
                    cos_v, sin_v = turns[2 * step], turns[2 * step + 1]
                    u, l = cos_v * u - sin_v * l, sin_v * u + cos_v * l
                    l = ahead(l, 1) if step < STEPS - 1 else ahead(l, BW - (STEPS - 1))
                turned[first, pl.ds(row, SUB), :] = u
                turned[second, pl.ds(row, SUB), :] = l

        write_back(first)
        write_back(second)
        return carry

    lax.fori_loop(0, order.shape[1] // 2, one_pair, 0)
    for slot in range(held):
        pltpu.make_async_copy(turned.at[slot], out.at[:, pl.ds(slot * BW, BW)], out_sem.at[slot]).wait()


def sum_over_rows(values):
    return lax.psum(values, "rows")


def body(matrix, plan):
    rows, width = matrix.shape
    count = width // BW * lax.axis_size("pairs")
    other = lax.ppermute(matrix, "pairs", [(0, 1), (1, 0)])
    smem = pl.BlockSpec(memory_space=pltpu.SMEM)
    vmem = pl.BlockSpec(memory_space=pltpu.VMEM)
    hbm = pl.BlockSpec(memory_space=pl.ANY)
    blocks = pltpu.VMEM((count, rows, BW), jnp.float32)
    params = pltpu.CompilerParams(vmem_limit_bytes=16 * 1024 * 1024)
    bands = pl.pallas_call(
        band_kernel,
        out_shape=jax.ShapeDtypeStruct((len(BANDS), count // 2, BW), jnp.float32),
        in_specs=[smem, hbm, hbm],
        out_specs=vmem,
        scratch_shapes=[blocks, pltpu.SemaphoreType.DMA((count,))],
        compiler_params=params,
        name="gram_bands",
    )(plan, matrix, other)
    bands = sum_over_rows(bands)
    return pl.pallas_call(
        turn_kernel,
        out_shape=jax.ShapeDtypeStruct((rows, width), jnp.float32),
        in_specs=[smem, vmem, hbm, hbm],
        out_specs=hbm,
        scratch_shapes=[
            blocks,
            blocks,
            pltpu.VMEM((2 * STEPS, count // 2, BW), jnp.float32),
            pltpu.SemaphoreType.DMA((count,)),
            pltpu.SemaphoreType.DMA((width // BW,)),
        ],
        compiler_params=params,
        name="turn_columns",
    )(plan, bands, matrix, other)


def solution(mesh):
    return jax.shard_map(
        body,
        mesh=mesh,
        in_specs=(P(("groups", "rows"), "pairs"), P()),
        out_specs=P(("groups", "rows"), "pairs"),
        check_vma=False,
    )
```

```python
import functools

import jax
import jax.numpy as jnp
from jax import lax
from jax.experimental import pallas as pl
from jax.experimental.pallas import tpu as pltpu
from jax.sharding import PartitionSpec as P

BW = 128
STEPS = 4
SUB = 8
BANDS = (
    [("uu", d) for d in range(STEPS)]
    + [("ll", d) for d in range(STEPS)]
    + [("ul", d) for d in range(STEPS)]
    + [("lu", d) for d in range(1, STEPS)]
)
SMEM = pl.BlockSpec(memory_space=pltpu.SMEM)
VMEM = pl.BlockSpec(memory_space=pltpu.VMEM)
HBM = pl.BlockSpec(memory_space=pl.ANY)
PARAMS = pltpu.CompilerParams(vmem_limit_bytes=24 * 1024 * 1024)


def ahead(values, d):
    return values if d == 0 else pltpu.roll(values, BW - d, 1)


def columns_of(slot):
    return pl.ds(pl.multiple_of(slot * BW, BW), BW)


def add(total, term):
    return term if total is None else total + term


def shift_kernel(mine, shifted, own):
    def one(slot, carry):
        columns = columns_of(slot)
        sums = [None] * STEPS
        for row in range(0, mine.shape[0], SUB):
            here = mine[pl.ds(row, SUB), columns]
            for d in range(STEPS):
                moved = ahead(here, d)
                sums[d] = add(sums[d], here * moved)
                if d:
                    shifted[d - 1, pl.ds(row, SUB), columns] = moved
        for d in range(STEPS):
            own[slot, d] = sums[d]
        return carry

    lax.fori_loop(0, mine.shape[1] // BW, one, 0)


def gram_kernel(order, mine, other, mine_shifted, own, bands, other_shifted, partial):
    rows = mine.shape[0]
    held = mine.shape[1] // BW
    pairs = order.shape[1] // 2
    me = lax.axis_index("pairs")

    def one_pair(pair, carry):
        first, second = order[0, 2 * pair], order[0, 2 * pair + 1]
        first_mine, second_mine = first // held == me, second // held == me

        def go(u_here, l_here):
            def load(here, slot, row):
                at = pl.ds(row, SUB), columns_of(slot)
                if here:
                    return [mine[at]] + [mine_shifted[(d, *at)] for d in range(STEPS - 1)]
                values = other[at]
                moved = [ahead(values, d) for d in range(STEPS)]
                if u_here or l_here:
                    for d in range(1, STEPS):
                        other_shifted[(d - 1, *at)] = moved[d]
                return moved

            u_slot, l_slot = first % held, second % held
            sums = {}
            for row in range(0, rows, SUB):
                u, l = load(u_here, u_slot, row), load(l_here, l_slot, row)
                for kind, d in BANDS:
                    if (kind == "uu" and u_here) or (kind == "ll" and l_here):
                        continue
                    term = (u if kind[0] == "u" else l)[0] * (u if kind[1] == "u" else l)[d]
                    sums[kind, d] = add(sums.get((kind, d)), term)
            for d in range(STEPS):
                if u_here:
                    sums["uu", d] = own[u_slot, d]
                if l_here:
                    sums["ll", d] = own[l_slot, d]
            for n, key in enumerate(BANDS):
                partial[n, pl.ds(pl.multiple_of(pair * SUB, SUB), SUB), :] = sums[key]

        for u_here in (True, False):
            for l_here in (True, False):
                pl.when((first_mine == u_here) & (second_mine == l_here))(
                    functools.partial(go, u_here, l_here)
                )
        return carry

    lax.fori_loop(0, pairs, one_pair, 0)
    for n in range(len(BANDS)):
        total = None
        for sub in range(SUB):
            total = add(total, partial[n, pl.ds(sub, pairs, stride=SUB), :])
        bands[n] = total


def rotation(upper, lower, cross):
    spread = lower - upper
    twice = jnp.where(spread >= 0, 2.0 * cross, -2.0 * cross)
    spread = jnp.abs(spread)
    scale = jnp.maximum(spread, jnp.abs(twice))
    zero = scale == 0
    scale = jnp.where(zero, 1.0, scale)
    x = jnp.where(zero, 1.0, spread / scale)
    y = twice / scale
    length = jnp.sqrt(x * x + y * y)
    cos_v = jnp.sqrt(0.5 + 0.5 * (x / length))
    sin_v = y / (2.0 * length * cos_v)
    return cos_v, sin_v


def jacobi_bands(g):
    turns = []
    for step in range(STEPS):
        cos_v, sin_v = rotation(g["uu", 0], g["ll", 0], g["ul", 0])
        turns.append((cos_v, sin_v))
        left = STEPS - 1 - step
        if left == 0:
            break
        new = {}
        for d in range(left + 1):
            cos_d, sin_d = ahead(cos_v, d), ahead(sin_v, d)
            uu, ll, ul = g["uu", d], g["ll", d], g["ul", d]
            lu = g["lu", d] if d else ul
            a, b = cos_v * uu - sin_v * lu, cos_v * ul - sin_v * ll
            e, f = sin_v * uu + cos_v * lu, sin_v * ul + cos_v * ll
            new["uu", d] = cos_d * a - sin_d * b
            new["ul", d] = sin_d * a + cos_d * b
            new["lu", d] = cos_d * e - sin_d * f
            new["ll", d] = sin_d * e + cos_d * f
        g = {}
        for d in range(left):
            g["uu", d] = new["uu", d]
            g["ll", d] = ahead(new["ll", d], 1)
            g["ul", d] = new["ul", d + 1]
            if d:
                g["lu", d] = ahead(new["ul", 0] if d == 1 else new["lu", d - 1], 1)
    return turns


def basis_bands(turns):
    x, y = {("u", 0): 1.0}, {("l", 0): 1.0}
    for step, (cos_v, sin_v) in enumerate(turns):
        if step:
            y = {(kind, i + 1): ahead(value, 1) for (kind, i), value in y.items()}
        keys = sorted(set(x) | set(y))
        new_x, new_y = {}, {}
        for key in keys:
            if key not in y:
                new_x[key], new_y[key] = cos_v * x[key], sin_v * x[key]
            elif key not in x:
                new_x[key], new_y[key] = -sin_v * y[key], cos_v * y[key]
            else:
                new_x[key] = cos_v * x[key] - sin_v * y[key]
                new_y[key] = sin_v * x[key] + cos_v * y[key]
        x, y = new_x, new_y
    return x, y


FACTORS = [(kind, i) for kind in "ul" for i in range(STEPS)]


def turn_kernel(order, bands, mine, other, mine_shifted, other_shifted, out, turned, factors, sem):
    rows = mine.shape[0]
    held = mine.shape[1] // BW
    pairs = order.shape[1] // 2
    me = lax.axis_index("pairs")
    x, y = basis_bands(jacobi_bands({key: bands[n] for n, key in enumerate(BANDS)}))
    for n, key in enumerate(FACTORS):
        factors[0, n] = x[key]
        factors[1, n] = y[key]

    def send(slot):
        return pltpu.make_async_copy(turned.at[slot], out.at[:, columns_of(slot)], sem.at[slot])

    def one_pair(pair, carry):
        first, second = order[0, 2 * pair], order[0, 2 * pair + 1]
        first_mine, second_mine = first // held == me, second // held == me

        def go(u_here, l_here):
            slots = {"u": first % held, "l": second % held}
            here = {"u": u_here, "l": l_here}
            scale = [
                [jnp.broadcast_to(factors[side, n, pl.ds(pair, 1), :], (SUB, BW)) for n in range(len(FACTORS))]
                for side in range(2)
            ]
            for row in range(0, rows, SUB):
                total = [None, None]
                for n, (kind, i) in enumerate(FACTORS):
                    at = pl.ds(row, SUB), columns_of(slots[kind])
                    if i:
                        value = (mine_shifted if here[kind] else other_shifted)[(i - 1, *at)]
                    else:
                        value = (mine if here[kind] else other)[at]
                    for side, kept in enumerate((u_here, l_here)):
                        if kept:
                            total[side] = add(total[side], scale[side][n] * value)
                if u_here:
                    turned[slots["u"], pl.ds(row, SUB), :] = total[0]
                if l_here:
                    turned[slots["l"], pl.ds(row, SUB), :] = ahead(total[1], BW - (STEPS - 1))
            for kind in "ul":
                if here[kind]:
                    send(slots[kind]).start()

        for u_here, l_here in ((True, True), (True, False), (False, True)):
            pl.when((first_mine == u_here) & (second_mine == l_here))(
                functools.partial(go, u_here, l_here)
            )
        return carry

    lax.fori_loop(0, pairs, one_pair, 0)
    for slot in range(held):
        send(slot).wait()


def sum_over_rows(values):
    size = lax.axis_size("rows")
    if size & (size - 1):
        return lax.psum(values, "rows")
    stride = 1
    while stride < size:
        radix = 4 if 4 * stride <= size else 2
        got = [
            lax.ppermute(values, "rows", [(i, i ^ (stride * m)) for i in range(size)])
            for m in range(1, radix)
        ]
        values = values + got[0]
        if radix == 4:
            values = values + (got[1] + got[2])
        stride *= radix
    return values


def body(matrix, plan):
    rows, width = matrix.shape
    held = width // BW
    pairs = held * lax.axis_size("pairs") // 2
    other = lax.ppermute(matrix, "pairs", [(0, 1), (1, 0)])
    moved = jax.ShapeDtypeStruct((STEPS - 1, rows, width), jnp.float32)
    mine_shifted, own = pl.pallas_call(
        shift_kernel,
        out_shape=[moved, jax.ShapeDtypeStruct((held, STEPS, SUB, BW), jnp.float32)],
        in_specs=[VMEM],
        out_specs=[VMEM, VMEM],
        compiler_params=PARAMS,
        cost_estimate=pl.CostEstimate(
            flops=8 * rows * width, bytes_accessed=4 * rows * width, transcendentals=0
        ),
        name="shift_own",
    )(matrix)
    bands, other_shifted = pl.pallas_call(
        gram_kernel,
        out_shape=[jax.ShapeDtypeStruct((len(BANDS), pairs, BW), jnp.float32), moved],
        in_specs=[SMEM, VMEM, VMEM, VMEM, VMEM],
        out_specs=[VMEM, VMEM],
        scratch_shapes=[pltpu.VMEM((len(BANDS), pairs * SUB, BW), jnp.float32)],
        compiler_params=PARAMS,
        name="gram_bands",
    )(plan, matrix, other, mine_shifted, own)
    bands = sum_over_rows(bands)
    return pl.pallas_call(
        turn_kernel,
        out_shape=jax.ShapeDtypeStruct((rows, width), jnp.float32),
        in_specs=[SMEM, VMEM, VMEM, VMEM, VMEM, VMEM],
        out_specs=HBM,
        scratch_shapes=[
            pltpu.VMEM((held, rows, BW), jnp.float32),
            pltpu.VMEM((2, len(FACTORS), pairs, BW), jnp.float32),
            pltpu.SemaphoreType.DMA((held,)),
        ],
        compiler_params=PARAMS,
        name="turn_columns",
    )(plan, bands, matrix, other, mine_shifted, other_shifted)


def solution(mesh):
    return jax.shard_map(
        body,
        mesh=mesh,
        in_specs=(P(("groups", "rows"), "pairs"), P()),
        out_specs=P(("groups", "rows"), "pairs"),
        check_vma=False,
    )
```

```python
import functools

import jax
import jax.numpy as jnp
from jax import lax
from jax.experimental import pallas as pl
from jax.experimental.pallas import tpu as pltpu
from jax.sharding import PartitionSpec as P

BW = 128
STEPS = 4
SUB = 8
BANDS = (
    [("uu", d) for d in range(STEPS)]
    + [("ll", d) for d in range(STEPS)]
    + [("ul", d) for d in range(STEPS)]
    + [("lu", d) for d in range(1, STEPS)]
)
SMEM = pl.BlockSpec(memory_space=pltpu.SMEM)
VMEM = pl.BlockSpec(memory_space=pltpu.VMEM)
HBM = pl.BlockSpec(memory_space=pl.ANY)
PARAMS = pltpu.CompilerParams(vmem_limit_bytes=24 * 1024 * 1024)


def ahead(values, d):
    return values if d == 0 else pltpu.roll(values, BW - d, 1)


def columns_of(slot):
    return pl.ds(pl.multiple_of(slot * BW, BW), BW)


def add(total, term):
    return term if total is None else total + term


def shift_kernel(mine, shifted, own):
    def one(slot, carry):
        columns = columns_of(slot)
        sums = [None] * STEPS
        for row in range(0, mine.shape[0], SUB):
            here = mine[pl.ds(row, SUB), columns]
            for d in range(STEPS):
                moved = ahead(here, d)
                sums[d] = add(sums[d], here * moved)
                if d:
                    shifted[d - 1, pl.ds(row, SUB), columns] = moved
        for d in range(STEPS):
            own[slot, d] = sums[d]
        return carry

    lax.fori_loop(0, mine.shape[1] // BW, one, 0)


def gram_kernel(order, mine, other, mine_shifted, own, bands, other_shifted, partial):
    rows = mine.shape[0]
    held = mine.shape[1] // BW
    pairs = order.shape[1] // 2
    me = lax.axis_index("pairs")

    def one_pair(pair, carry):
        first, second = order[0, 2 * pair], order[0, 2 * pair + 1]
        first_mine, second_mine = first // held == me, second // held == me

        def go(u_here, l_here):
            def load(here, slot, row):
                at = pl.ds(row, SUB), columns_of(slot)
                if here:
                    return [mine[at]] + [mine_shifted[(d, *at)] for d in range(STEPS - 1)]
                values = other[at]
                moved = [ahead(values, d) for d in range(STEPS)]
                if u_here or l_here:
                    for d in range(1, STEPS):
                        other_shifted[(d - 1, *at)] = moved[d]
                return moved

            u_slot, l_slot = first % held, second % held
            sums = {}
            for row in range(0, rows, SUB):
                u, l = load(u_here, u_slot, row), load(l_here, l_slot, row)
                for kind, d in BANDS:
                    if (kind == "uu" and u_here) or (kind == "ll" and l_here):
                        continue
                    term = (u if kind[0] == "u" else l)[0] * (u if kind[1] == "u" else l)[d]
                    sums[kind, d] = add(sums.get((kind, d)), term)
            for d in range(STEPS):
                if u_here:
                    sums["uu", d] = own[u_slot, d]
                if l_here:
                    sums["ll", d] = own[l_slot, d]
            for n, key in enumerate(BANDS):
                partial[n, pl.ds(pl.multiple_of(pair * SUB, SUB), SUB), :] = sums[key]

        for u_here in (True, False):
            for l_here in (True, False):
                pl.when((first_mine == u_here) & (second_mine == l_here))(
                    functools.partial(go, u_here, l_here)
                )
        return carry

    lax.fori_loop(0, pairs, one_pair, 0)
    for n in range(len(BANDS)):
        total = None
        for sub in range(SUB):
            total = add(total, partial[n, pl.ds(sub, pairs, stride=SUB), :])
        bands[n] = total


def rotation(upper, lower, cross):
    spread = lower - upper
    twice = jnp.where(spread >= 0, 2.0 * cross, -2.0 * cross)
    spread = jnp.abs(spread)
    scale = jnp.maximum(spread, jnp.abs(twice))
    zero = scale == 0
    scale = jnp.where(zero, 1.0, scale)
    x = jnp.where(zero, 1.0, spread / scale)
    y = twice / scale
    length = jnp.sqrt(x * x + y * y)
    cos_v = jnp.sqrt(0.5 + 0.5 * (x / length))
    sin_v = y / (2.0 * length * cos_v)
    return cos_v, sin_v


def jacobi_bands(g):
    turns = []
    for step in range(STEPS):
        cos_v, sin_v = rotation(g["uu", 0], g["ll", 0], g["ul", 0])
        turns.append((cos_v, sin_v))
        left = STEPS - 1 - step
        if left == 0:
            break
        new = {}
        for d in range(left + 1):
            cos_d, sin_d = ahead(cos_v, d), ahead(sin_v, d)
            uu, ll, ul = g["uu", d], g["ll", d], g["ul", d]
            lu = g["lu", d] if d else ul
            a, b = cos_v * uu - sin_v * lu, cos_v * ul - sin_v * ll
            e, f = sin_v * uu + cos_v * lu, sin_v * ul + cos_v * ll
            new["uu", d] = cos_d * a - sin_d * b
            new["ul", d] = sin_d * a + cos_d * b
            new["lu", d] = cos_d * e - sin_d * f
            new["ll", d] = sin_d * e + cos_d * f
        g = {}
        for d in range(left):
            g["uu", d] = new["uu", d]
            g["ll", d] = ahead(new["ll", d], 1)
            g["ul", d] = new["ul", d + 1]
            if d:
                g["lu", d] = ahead(new["ul", 0] if d == 1 else new["lu", d - 1], 1)
    return turns


def basis_bands(turns):
    x, y = {("u", 0): 1.0}, {("l", 0): 1.0}
    for step, (cos_v, sin_v) in enumerate(turns):
        if step:
            y = {(kind, i + 1): ahead(value, 1) for (kind, i), value in y.items()}
        keys = sorted(set(x) | set(y))
        new_x, new_y = {}, {}
        for key in keys:
            if key not in y:
                new_x[key], new_y[key] = cos_v * x[key], sin_v * x[key]
            elif key not in x:
                new_x[key], new_y[key] = -sin_v * y[key], cos_v * y[key]
            else:
                new_x[key] = cos_v * x[key] - sin_v * y[key]
                new_y[key] = sin_v * x[key] + cos_v * y[key]
        x, y = new_x, new_y
    return x, y


FACTORS = [(kind, i) for kind in "ul" for i in range(STEPS)]


def turn_kernel(order, bands, mine, other, mine_shifted, other_shifted, out, turned, factors, sem):
    rows = mine.shape[0]
    held = mine.shape[1] // BW
    pairs = order.shape[1] // 2
    me = lax.axis_index("pairs")
    x, y = basis_bands(jacobi_bands({key: bands[n] for n, key in enumerate(BANDS)}))
    for n, key in enumerate(FACTORS):
        factors[0, n] = x[key]
        factors[1, n] = y[key]

    def send(slot):
        return pltpu.make_async_copy(turned.at[slot], out.at[:, columns_of(slot)], sem.at[slot])

    def one_pair(pair, carry):
        first, second = order[0, 2 * pair], order[0, 2 * pair + 1]
        first_mine, second_mine = first // held == me, second // held == me

        def go(u_here, l_here):
            slots = {"u": first % held, "l": second % held}
            here = {"u": u_here, "l": l_here}
            scale = [
                [jnp.broadcast_to(factors[side, n, pl.ds(pair, 1), :], (SUB, BW)) for n in range(len(FACTORS))]
                for side in range(2)
            ]
            for row in range(0, rows, SUB):
                total = [None, None]
                for n, (kind, i) in enumerate(FACTORS):
                    at = pl.ds(row, SUB), columns_of(slots[kind])
                    if i:
                        value = (mine_shifted if here[kind] else other_shifted)[(i - 1, *at)]
                    else:
                        value = (mine if here[kind] else other)[at]
                    for side, kept in enumerate((u_here, l_here)):
                        if kept:
                            total[side] = add(total[side], scale[side][n] * value)
                if u_here:
                    turned[slots["u"], pl.ds(row, SUB), :] = total[0]
                if l_here:
                    turned[slots["l"], pl.ds(row, SUB), :] = ahead(total[1], BW - (STEPS - 1))
            for kind in "ul":
                if here[kind]:
                    send(slots[kind]).start()

        for u_here, l_here in ((True, True), (True, False), (False, True)):
            pl.when((first_mine == u_here) & (second_mine == l_here))(
                functools.partial(go, u_here, l_here)
            )
        return carry

    lax.fori_loop(0, pairs, one_pair, 0)
    for slot in range(held):
        send(slot).wait()


def sum_over_rows(values):
    return jnp.sum(lax.all_gather(values, "rows"), axis=0)


def body(matrix, plan):
    rows, width = matrix.shape
    held = width // BW
    pairs = held * lax.axis_size("pairs") // 2
    other = lax.ppermute(matrix, "pairs", [(0, 1), (1, 0)])
    moved = jax.ShapeDtypeStruct((STEPS - 1, rows, width), jnp.float32)
    mine_shifted, own = pl.pallas_call(
        shift_kernel,
        out_shape=[moved, jax.ShapeDtypeStruct((held, STEPS, SUB, BW), jnp.float32)],
        in_specs=[VMEM],
        out_specs=[VMEM, VMEM],
        compiler_params=PARAMS,
        cost_estimate=pl.CostEstimate(
            flops=8 * rows * width, bytes_accessed=4 * rows * width, transcendentals=0
        ),
        name="shift_own",
    )(matrix)
    bands, other_shifted = pl.pallas_call(
        gram_kernel,
        out_shape=[jax.ShapeDtypeStruct((len(BANDS), pairs, BW), jnp.float32), moved],
        in_specs=[SMEM, VMEM, VMEM, VMEM, VMEM],
        out_specs=[VMEM, VMEM],
        scratch_shapes=[pltpu.VMEM((len(BANDS), pairs * SUB, BW), jnp.float32)],
        compiler_params=PARAMS,
        name="gram_bands",
    )(plan, matrix, other, mine_shifted, own)
    bands = sum_over_rows(bands)
    return pl.pallas_call(
        turn_kernel,
        out_shape=jax.ShapeDtypeStruct((rows, width), jnp.float32),
        in_specs=[SMEM, VMEM, VMEM, VMEM, VMEM, VMEM],
        out_specs=HBM,
        scratch_shapes=[
            pltpu.VMEM((held, rows, BW), jnp.float32),
            pltpu.VMEM((2, len(FACTORS), pairs, BW), jnp.float32),
            pltpu.SemaphoreType.DMA((held,)),
        ],
        compiler_params=PARAMS,
        name="turn_columns",
    )(plan, bands, matrix, other, mine_shifted, other_shifted)


def solution(mesh):
    return jax.shard_map(
        body,
        mesh=mesh,
        in_specs=(P(("groups", "rows"), "pairs"), P()),
        out_specs=P(("groups", "rows"), "pairs"),
        check_vma=False,
    )
```

```python
import functools

import jax
import jax.numpy as jnp
from jax import lax
from jax.experimental import pallas as pl
from jax.experimental.pallas import tpu as pltpu
from jax.sharding import PartitionSpec as P

BW = 128
STEPS = 4
SUB = 8
BANDS = (
    [("uu", d) for d in range(STEPS)]
    + [("ll", d) for d in range(STEPS)]
    + [("ul", d) for d in range(STEPS)]
    + [("lu", d) for d in range(1, STEPS)]
)
SMEM = pl.BlockSpec(memory_space=pltpu.SMEM)
VMEM = pl.BlockSpec(memory_space=pltpu.VMEM)
BAND_ROWS = 16
HBM = pl.BlockSpec(memory_space=pl.ANY)
PARAMS = pltpu.CompilerParams(vmem_limit_bytes=24 * 1024 * 1024)


def ahead(values, d):
    return values if d == 0 else pltpu.roll(values, BW - d, 1)


def columns_of(slot):
    return pl.ds(pl.multiple_of(slot * BW, BW), BW)


def add(total, term):
    return term if total is None else total + term


def share_pairs(plan, order, held):
    pairs = plan.shape[1] // 2

    def one(pair, carry):
        straddling, taken = carry
        first, second = plan[0, 2 * pair], plan[0, 2 * pair + 1]
        inside = first // held == second // held
        core = jnp.where(inside, first // held, straddling % 2)
        place = jnp.where(core == 0, taken, pairs // 2 + pair - taken)
        order[0, 2 * place] = first
        order[0, 2 * place + 1] = second
        return straddling + jnp.where(inside, 0, 1), taken + jnp.where(core == 0, 1, 0)

    lax.fori_loop(0, pairs, one, (jnp.int32(0), jnp.int32(0)))


def shift_kernel(plan, matrix, order, shifted, own, plan_here, sem, plan_sem):
    rows = matrix.shape[0]
    held = matrix.shape[1] // BW

    def fetch(slot):
        columns = columns_of(slot)
        return pltpu.make_async_copy(matrix.at[:, columns], shifted.at[0, :, columns], sem.at[slot])

    for slot in range(held):
        fetch(slot).start()
    plan_copy = pltpu.make_async_copy(plan, plan_here, plan_sem)
    plan_copy.start()

    def one(slot, carry):
        fetch(slot).wait()
        columns = columns_of(slot)
        sums = [None] * STEPS
        for row in range(0, rows, SUB):
            here = shifted[0, pl.ds(row, SUB), columns]
            for d in range(STEPS):
                moved = ahead(here, d)
                sums[d] = add(sums[d], here * moved)
                if d:
                    shifted[d, pl.ds(row, SUB), columns] = moved
        for d in range(STEPS):
            own[slot, d] = sums[d]
        return carry

    lax.fori_loop(0, held, one, 0)
    plan_copy.wait()
    share_pairs(plan_here, order, held)


def gram_kernel(order, other, mine_shifted, own, bands, other_shifted, partial):
    rows, width = other.shape
    held = width // BW
    pairs = order.shape[1] // 4
    me = lax.axis_index("pairs")

    def one_pair(pair, carry):
        first, second = order[0, 2 * (me * pairs + pair)], order[0, 2 * (me * pairs + pair) + 1]
        first_mine, second_mine = first // held == me, second // held == me

        def go(u_here, l_here):
            def load(here, slot, row):
                at = pl.ds(row, SUB), columns_of(slot)
                if here:
                    return [mine_shifted[(d, *at)] for d in range(STEPS)]
                values = other[at]
                moved = [ahead(values, d) for d in range(STEPS)]
                for d in range(1, STEPS):
                    other_shifted[(d - 1, *at)] = moved[d]
                return moved

            u_slot, l_slot = first % held, second % held
            sums = {}
            for row in range(0, rows, SUB):
                u, l = load(u_here, u_slot, row), load(l_here, l_slot, row)
                for kind, d in BANDS:
                    if (kind == "uu" and u_here) or (kind == "ll" and l_here):
                        continue
                    term = (u if kind[0] == "u" else l)[0] * (u if kind[1] == "u" else l)[d]
                    sums[kind, d] = add(sums.get((kind, d)), term)
            for d in range(STEPS):
                if u_here:
                    sums["uu", d] = own[u_slot, d]
                if l_here:
                    sums["ll", d] = own[l_slot, d]
            for n, key in enumerate(BANDS):
                at = pl.multiple_of((n * pairs + pair) * SUB, SUB)
                partial[pl.ds(at, SUB), :] = sums[key]

        for u_here, l_here in ((True, True), (True, False), (False, True)):
            pl.when((first_mine == u_here) & (second_mine == l_here))(
                functools.partial(go, u_here, l_here)
            )
        return carry

    lax.fori_loop(0, pairs, one_pair, 0)
    used = len(BANDS) * pairs
    partial[pl.ds(used * SUB, (BAND_ROWS * pairs - used) * SUB), :] = jnp.zeros(
        ((BAND_ROWS * pairs - used) * SUB, BW), jnp.float32
    )
    for row in range(0, BAND_ROWS * pairs, SUB):
        total = None
        for sub in range(SUB):
            total = add(total, partial[pl.ds(row * SUB + sub, SUB, stride=SUB), :])
        bands[pl.ds(row, SUB), :] = total


def shift_rest_kernel(order, bands, other, kept, other_shifted):
    held = other.shape[1] // BW
    pairs = order.shape[1] // 4
    me = lax.axis_index("pairs")
    kept[...] = bands[...]

    def one(i, carry):
        block = order[0, 2 * (1 - me) * pairs + i]
        partner = order[0, 2 * (1 - me) * pairs + i + 1 - 2 * (i % 2)]

        @pl.when((block // held != me) & (partner // held == me))
        def _():
            columns = columns_of(block % held)
            for row in range(0, other.shape[0], SUB):
                here = other[pl.ds(row, SUB), columns]
                for d in range(1, STEPS):
                    other_shifted[d - 1, pl.ds(row, SUB), columns] = ahead(here, d)

        return carry

    lax.fori_loop(0, 2 * pairs, one, 0)


def rotation(upper, lower, cross):
    spread = lower - upper
    twice = jnp.where(spread >= 0, 2.0 * cross, -2.0 * cross)
    spread = jnp.abs(spread)
    scale = jnp.maximum(spread, jnp.abs(twice))
    zero = scale == 0
    scale = jnp.where(zero, 1.0, scale)
    x = jnp.where(zero, 1.0, spread / scale)
    y = twice / scale
    length = jnp.sqrt(x * x + y * y)
    cos_v = jnp.sqrt(0.5 + 0.5 * (x / length))
    sin_v = y / (2.0 * length * cos_v)
    return cos_v, sin_v


def jacobi_bands(g):
    turns = []
    for step in range(STEPS):
        cos_v, sin_v = rotation(g["uu", 0], g["ll", 0], g["ul", 0])
        turns.append((cos_v, sin_v))
        left = STEPS - 1 - step
        if left == 0:
            break
        new = {}
        for d in range(left + 1):
            cos_d, sin_d = ahead(cos_v, d), ahead(sin_v, d)
            uu, ll, ul = g["uu", d], g["ll", d], g["ul", d]
            lu = g["lu", d] if d else ul
            a, b = cos_v * uu - sin_v * lu, cos_v * ul - sin_v * ll
            e, f = sin_v * uu + cos_v * lu, sin_v * ul + cos_v * ll
            new["uu", d] = cos_d * a - sin_d * b
            new["ul", d] = sin_d * a + cos_d * b
            new["lu", d] = cos_d * e - sin_d * f
            new["ll", d] = sin_d * e + cos_d * f
        g = {}
        for d in range(left):
            g["uu", d] = new["uu", d]
            g["ll", d] = ahead(new["ll", d], 1)
            g["ul", d] = new["ul", d + 1]
            if d:
                g["lu", d] = ahead(new["ul", 0] if d == 1 else new["lu", d - 1], 1)
    return turns


def basis_bands(turns):
    x, y = {("u", 0): 1.0}, {("l", 0): 1.0}
    for step, (cos_v, sin_v) in enumerate(turns):
        if step:
            y = {(kind, i + 1): ahead(value, 1) for (kind, i), value in y.items()}
        keys = sorted(set(x) | set(y))
        new_x, new_y = {}, {}
        for key in keys:
            if key not in y:
                new_x[key], new_y[key] = cos_v * x[key], sin_v * x[key]
            elif key not in x:
                new_x[key], new_y[key] = -sin_v * y[key], cos_v * y[key]
            else:
                new_x[key] = cos_v * x[key] - sin_v * y[key]
                new_y[key] = sin_v * x[key] + cos_v * y[key]
        x, y = new_x, new_y
    return x, y


FACTORS = [(kind, i) for kind in "ul" for i in range(STEPS)]


def turn_kernel(
    order, summed, passed, other, mine_shifted, own_half, other_half, out, turned, bands, factors, sem
):
    rows, width = other.shape
    held = width // BW
    pairs = order.shape[1] // 4
    me = lax.axis_index("pairs")
    for n in range(len(BANDS)):
        mine, theirs = summed[pl.ds(n * pairs, pairs), :], passed[pl.ds(n * pairs, pairs), :]
        bands[n, pl.ds(0, pairs), :] = jnp.where(me == 0, mine, theirs)
        bands[n, pl.ds(pairs, pairs), :] = jnp.where(me == 0, theirs, mine)
    x, y = basis_bands(jacobi_bands({key: bands[n] for n, key in enumerate(BANDS)}))
    for n, key in enumerate(FACTORS):
        factors[0, n] = x[key]
        factors[1, n] = y[key]

    def send(slot):
        return pltpu.make_async_copy(turned.at[slot], out.at[:, columns_of(slot)], sem.at[slot])

    def one_pair(other_shifted, cases, base, i, carry):
        pair = base + i
        first, second = order[0, 2 * pair], order[0, 2 * pair + 1]
        first_mine, second_mine = first // held == me, second // held == me

        def go(u_here, l_here):
            slots = {"u": first % held, "l": second % held}
            here = {"u": u_here, "l": l_here}
            scale = [
                [jnp.broadcast_to(factors[side, n, pl.ds(pair, 1), :], (SUB, BW)) for n in range(len(FACTORS))]
                for side in range(2)
            ]
            for row in range(0, rows, SUB):
                total = [None, None]
                for n, (kind, i) in enumerate(FACTORS):
                    at = pl.ds(row, SUB), columns_of(slots[kind])
                    if here[kind]:
                        value = mine_shifted[(i, *at)]
                    else:
                        value = other_shifted[(i - 1, *at)] if i else other[at]
                    for side, kept in enumerate((u_here, l_here)):
                        if kept:
                            total[side] = add(total[side], scale[side][n] * value)
                if u_here:
                    turned[slots["u"], pl.ds(row, SUB), :] = total[0]
                if l_here:
                    turned[slots["l"], pl.ds(row, SUB), :] = ahead(total[1], BW - (STEPS - 1))
            for kind in "ul":
                if here[kind]:
                    send(slots[kind]).start()

        for u_here, l_here in cases:
            pl.when((first_mine == u_here) & (second_mine == l_here))(
                functools.partial(go, u_here, l_here)
            )
        return carry

    straddling = ((True, False), (False, True))
    lax.fori_loop(0, pairs, functools.partial(one_pair, own_half, ((True, True), *straddling), me * pairs), 0)
    lax.fori_loop(0, pairs, functools.partial(one_pair, other_half, straddling, (1 - me) * pairs), 0)
    for slot in range(held):
        send(slot).wait()


def sum_over_rows(values, first):
    size = lax.axis_size("rows")
    if size & (size - 1):
        return lax.psum(values, "rows")
    got = [
        lax.ppermute(values, "rows", [(i, i ^ m) for i in range(size)]) for m in (1, 2, 3) if m < size
    ]
    summed = first
    if got:
        summed = summed + got[0]
    if got[1:]:
        summed = summed + (got[1] + got[2])
    stride = 4
    while stride < size:
        summed = summed + lax.ppermute(summed, "rows", [(i, i ^ stride) for i in range(size)])
        stride *= 2
    return summed


def body(matrix, plan):
    rows, width = matrix.shape
    held = width // BW
    pairs = held // 2
    swap = [(0, 1), (1, 0)]
    other = lax.ppermute(matrix, "pairs", swap)
    cost = pl.CostEstimate(flops=30 * rows * width, bytes_accessed=8 * rows * width, transcendentals=0)
    columns = jax.ShapeDtypeStruct((STEPS - 1, rows, width), jnp.float32)
    bands_shape = jax.ShapeDtypeStruct((BAND_ROWS * pairs, BW), jnp.float32)
    order, mine_shifted, own = pl.pallas_call(
        shift_kernel,
        out_shape=[
            jax.ShapeDtypeStruct(plan.shape, plan.dtype),
            jax.ShapeDtypeStruct((STEPS, rows, width), jnp.float32),
            jax.ShapeDtypeStruct((held, STEPS, SUB, BW), jnp.float32),
        ],
        in_specs=[HBM, HBM],
        out_specs=[SMEM, VMEM, VMEM],
        scratch_shapes=[
            pltpu.SMEM(plan.shape, plan.dtype),
            pltpu.SemaphoreType.DMA((held,)),
            pltpu.SemaphoreType.DMA,
        ],
        compiler_params=PARAMS,
        cost_estimate=cost,
        name="shift_own",
    )(
        pltpu.with_memory_space_constraint(plan, pltpu.HBM),
        pltpu.with_memory_space_constraint(matrix, pltpu.HBM),
    )
    bands, own_half = pl.pallas_call(
        gram_kernel,
        out_shape=[bands_shape, columns],
        in_specs=[SMEM, VMEM, VMEM, VMEM],
        out_specs=[VMEM, VMEM],
        scratch_shapes=[pltpu.VMEM((BAND_ROWS * pairs * SUB, BW), jnp.float32)],
        compiler_params=PARAMS,
        cost_estimate=cost,
        name="gram_bands",
    )(order, other, mine_shifted, own)
    kept, other_half = pl.pallas_call(
        shift_rest_kernel,
        out_shape=[bands_shape, columns],
        in_specs=[SMEM, VMEM, VMEM],
        out_specs=[VMEM, VMEM],
        compiler_params=PARAMS,
        cost_estimate=cost,
        name="shift_rest",
    )(order, bands, other)
    summed = sum_over_rows(bands, kept)
    passed = lax.ppermute(summed, "pairs", swap)
    return pl.pallas_call(
        turn_kernel,
        out_shape=jax.ShapeDtypeStruct((rows, width), jnp.float32),
        in_specs=[SMEM] + [VMEM] * 6,
        out_specs=HBM,
        scratch_shapes=[
            pltpu.VMEM((held, rows, BW), jnp.float32),
            pltpu.VMEM((len(BANDS), 2 * pairs, BW), jnp.float32),
            pltpu.VMEM((2, len(FACTORS), 2 * pairs, BW), jnp.float32),
            pltpu.SemaphoreType.DMA((held,)),
        ],
        compiler_params=PARAMS,
        name="turn_columns",
    )(order, summed, passed, other, mine_shifted, own_half, other_half)


def solution(mesh):
    return jax.shard_map(
        body,
        mesh=mesh,
        in_specs=(P(("groups", "rows"), "pairs"), P()),
        out_specs=P(("groups", "rows"), "pairs"),
        check_vma=False,
    )
```

```python
import functools

import jax
import jax.numpy as jnp
from jax import lax
from jax.experimental import pallas as pl
from jax.experimental.pallas import tpu as pltpu
from jax.sharding import PartitionSpec as P

BW = 128
STEPS = 4
SUB = 8
SUMMER = 1
BANDS = (
    [("uu", d) for d in range(STEPS)]
    + [("ll", d) for d in range(STEPS)]
    + [("ul", d) for d in range(STEPS)]
    + [("lu", d) for d in range(1, STEPS)]
)
SMEM = pl.BlockSpec(memory_space=pltpu.SMEM)
VMEM = pl.BlockSpec(memory_space=pltpu.VMEM)
HBM = pl.BlockSpec(memory_space=pl.ANY)
PARAMS = pltpu.CompilerParams(vmem_limit_bytes=24 * 1024 * 1024)


def ahead(values, d):
    return values if d == 0 else pltpu.roll(values, BW - d, 1)


def columns_of(slot):
    return pl.ds(pl.multiple_of(slot * BW, BW), BW)


def core_of(block, held):
    return lax.div(block, jnp.int32(held))


def slot_of(block, held):
    return lax.rem(block, jnp.int32(held))


def add(total, term):
    return term if total is None else total + term


def shift_kernel(plan, matrix, order, shifted, own, sem, plan_sem):
    rows = matrix.shape[0]
    held = matrix.shape[1] // BW

    def fetch(slot):
        columns = columns_of(slot)
        return pltpu.make_async_copy(matrix.at[:, columns], shifted.at[0, :, columns], sem.at[slot])

    order_copy = pltpu.make_async_copy(plan, order, plan_sem)
    for slot in range(held):
        fetch(slot).start()
    order_copy.start()

    def one(slot, carry):
        fetch(slot).wait()
        columns = columns_of(slot)
        sums = [None] * STEPS
        for row in range(0, rows, SUB):
            here = shifted[0, pl.ds(row, SUB), columns]
            for d in range(STEPS):
                moved = ahead(here, d)
                sums[d] = add(sums[d], here * moved)
                if d:
                    shifted[d, pl.ds(row, SUB), columns] = moved
        for d in range(STEPS):
            own[slot, d] = sums[d]
        return carry

    lax.fori_loop(0, held, one, 0)
    order_copy.wait()


def gram_kernel(order, other, mine_shifted, own, bands, other_shifted, partial):
    rows, width = other.shape
    held = width // BW
    pairs = order.shape[1] // 2
    me = lax.axis_index("pairs")

    def one_pair(pair, carry):
        first, second = order[0, 2 * pair], order[0, 2 * pair + 1]
        first_mine, second_mine = core_of(first, held) == me, core_of(second, held) == me

        def go(u_here, l_here):
            def load(here, slot, row):
                at = pl.ds(row, SUB), columns_of(slot)
                if here:
                    return [mine_shifted[(d, *at)] for d in range(STEPS)]
                values = other[at]
                moved = [ahead(values, d) for d in range(STEPS)]
                if u_here or l_here:
                    for d in range(1, STEPS):
                        other_shifted[(d - 1, *at)] = moved[d]
                return moved

            u_slot, l_slot = slot_of(first, held), slot_of(second, held)
            sums = {}
            for row in range(0, rows, SUB):
                u, l = load(u_here, u_slot, row), load(l_here, l_slot, row)
                for kind, d in BANDS:
                    if (kind == "uu" and u_here) or (kind == "ll" and l_here):
                        continue
                    term = (u if kind[0] == "u" else l)[0] * (u if kind[1] == "u" else l)[d]
                    sums[kind, d] = add(sums.get((kind, d)), term)
            for d in range(STEPS):
                if u_here:
                    sums["uu", d] = own[u_slot, d]
                if l_here:
                    sums["ll", d] = own[l_slot, d]
            for n, key in enumerate(BANDS):
                partial[n, pl.ds(pl.multiple_of(pair * SUB, SUB), SUB), :] = sums[key]

        for u_here in (True, False):
            for l_here in (True, False):
                pl.when((first_mine == u_here) & (second_mine == l_here))(
                    functools.partial(go, u_here, l_here)
                )
        return carry

    lax.fori_loop(0, pairs, one_pair, 0)
    for n in range(len(BANDS)):
        total = None
        for sub in range(SUB):
            total = add(total, partial[n, pl.ds(sub, pairs, stride=SUB), :])
        bands[n] = total


def rotation(upper, lower, cross):
    spread = lower - upper
    twice = jnp.where(spread >= 0, 2.0 * cross, -2.0 * cross)
    spread = jnp.abs(spread)
    scale = jnp.maximum(spread, jnp.abs(twice))
    zero = scale == 0
    scale = jnp.where(zero, 1.0, scale)
    x = jnp.where(zero, 1.0, spread / scale)
    y = twice / scale
    length = jnp.sqrt(x * x + y * y)
    cos_v = jnp.sqrt(0.5 + 0.5 * (x / length))
    sin_v = y / (2.0 * length * cos_v)
    return cos_v, sin_v


def jacobi_bands(g):
    turns = []
    for step in range(STEPS):
        cos_v, sin_v = rotation(g["uu", 0], g["ll", 0], g["ul", 0])
        turns.append((cos_v, sin_v))
        left = STEPS - 1 - step
        if left == 0:
            break
        new = {}
        for d in range(left + 1):
            cos_d, sin_d = ahead(cos_v, d), ahead(sin_v, d)
            uu, ll, ul = g["uu", d], g["ll", d], g["ul", d]
            lu = g["lu", d] if d else ul
            a, b = cos_v * uu - sin_v * lu, cos_v * ul - sin_v * ll
            e, f = sin_v * uu + cos_v * lu, sin_v * ul + cos_v * ll
            new["uu", d] = cos_d * a - sin_d * b
            new["ul", d] = sin_d * a + cos_d * b
            new["lu", d] = cos_d * e - sin_d * f
            new["ll", d] = sin_d * e + cos_d * f
        g = {}
        for d in range(left):
            g["uu", d] = new["uu", d]
            g["ll", d] = ahead(new["ll", d], 1)
            g["ul", d] = new["ul", d + 1]
            if d:
                g["lu", d] = ahead(new["ul", 0] if d == 1 else new["lu", d - 1], 1)
    return turns


def basis_bands(turns):
    x, y = {("u", 0): 1.0}, {("l", 0): 1.0}
    for step, (cos_v, sin_v) in enumerate(turns):
        if step:
            y = {(kind, i + 1): ahead(value, 1) for (kind, i), value in y.items()}
        keys = sorted(set(x) | set(y))
        new_x, new_y = {}, {}
        for key in keys:
            if key not in y:
                new_x[key], new_y[key] = cos_v * x[key], sin_v * x[key]
            elif key not in x:
                new_x[key], new_y[key] = -sin_v * y[key], cos_v * y[key]
            else:
                new_x[key] = cos_v * x[key] - sin_v * y[key]
                new_y[key] = sin_v * x[key] + cos_v * y[key]
        x, y = new_x, new_y
    return x, y


FACTORS = [(kind, i) for kind in "ul" for i in range(STEPS)]


def turn_kernel(
    plan, summed, passed, other, mine_shifted, other_shifted, out, turned, factors, order, sem, plan_sem
):
    rows, width = other.shape
    held = width // BW
    pairs = plan.shape[1] // 2
    me = lax.axis_index("pairs")
    plan_copy = pltpu.make_async_copy(plan, order, plan_sem)
    plan_copy.start()
    bands = {key: jnp.where(me == SUMMER, summed[n], passed[n]) for n, key in enumerate(BANDS)}
    x, y = basis_bands(jacobi_bands(bands))
    for n, key in enumerate(FACTORS):
        factors[0, n] = x[key]
        factors[1, n] = y[key]
    plan_copy.wait()

    def send(slot):
        return pltpu.make_async_copy(turned.at[slot], out.at[:, columns_of(slot)], sem.at[slot])

    def one_pair(pair, carry):
        first, second = order[0, 2 * pair], order[0, 2 * pair + 1]
        first_mine, second_mine = core_of(first, held) == me, core_of(second, held) == me

        def go(u_here, l_here):
            slots = {"u": slot_of(first, held), "l": slot_of(second, held)}
            here = {"u": u_here, "l": l_here}
            scale = [
                [jnp.broadcast_to(factors[side, n, pl.ds(pair, 1), :], (SUB, BW)) for n in range(len(FACTORS))]
                for side in range(2)
            ]
            for row in range(0, rows, SUB):
                total = [None, None]
                for n, (kind, i) in enumerate(FACTORS):
                    at = pl.ds(row, SUB), columns_of(slots[kind])
                    if here[kind]:
                        value = mine_shifted[(i, *at)]
                    else:
                        value = other_shifted[(i - 1, *at)] if i else other[at]
                    for side, kept in enumerate((u_here, l_here)):
                        if kept:
                            total[side] = add(total[side], scale[side][n] * value)
                if u_here:
                    turned[slots["u"], pl.ds(row, SUB), :] = total[0]
                if l_here:
                    turned[slots["l"], pl.ds(row, SUB), :] = ahead(total[1], BW - (STEPS - 1))
            for kind in "ul":
                if here[kind]:
                    send(slots[kind]).start()

        for u_here, l_here in ((True, True), (True, False), (False, True)):
            pl.when((first_mine == u_here) & (second_mine == l_here))(
                functools.partial(go, u_here, l_here)
            )
        return carry

    lax.fori_loop(0, pairs, one_pair, 0)
    for slot in range(held):
        send(slot).wait()


def exchange(values, stride):
    size, cores = lax.axis_size("rows"), lax.axis_size("pairs")
    route = [
        (i * cores + core, (i ^ stride if core == SUMMER else i) * cores + core)
        for i in range(size)
        for core in range(cores)
    ]
    return lax.ppermute(values, ("rows", "pairs"), route)


def sum_over_rows(values):
    size = lax.axis_size("rows")
    if size & (size - 1):
        return lax.psum(values, "rows")
    got = [exchange(values, stride) for stride in (1, 2, 3) if stride < size]
    if got:
        values = values + got[0]
    if got[1:]:
        values = values + (got[1] + got[2])
    stride = 4
    while stride < size:
        values = values + exchange(values, stride)
        stride *= 2
    return values


def body(matrix, plan):
    rows, width = matrix.shape
    held = width // BW
    pairs = held * lax.axis_size("pairs") // 2
    blocks = len(BANDS)
    swap = [(0, 1), (1, 0)]
    other = lax.ppermute(matrix, "pairs", swap)
    cost = pl.CostEstimate(flops=30 * rows * width, bytes_accessed=8 * rows * width, transcendentals=0)
    order, mine_shifted, own = pl.pallas_call(
        shift_kernel,
        out_shape=[
            jax.ShapeDtypeStruct(plan.shape, plan.dtype),
            jax.ShapeDtypeStruct((STEPS, rows, width), jnp.float32),
            jax.ShapeDtypeStruct((held, STEPS, SUB, BW), jnp.float32),
        ],
        in_specs=[HBM, HBM],
        out_specs=[VMEM, VMEM, VMEM],
        scratch_shapes=[pltpu.SemaphoreType.DMA((held,)), pltpu.SemaphoreType.DMA],
        compiler_params=PARAMS,
        cost_estimate=cost,
        name="shift_own",
    )(
        pltpu.with_memory_space_constraint(plan, pltpu.HBM),
        pltpu.with_memory_space_constraint(matrix, pltpu.HBM),
    )

    bands, other_shifted = pl.pallas_call(
        gram_kernel,
        out_shape=[
            jax.ShapeDtypeStruct((blocks, pairs, BW), jnp.float32),
            jax.ShapeDtypeStruct((STEPS - 1, rows, width), jnp.float32),
        ],
        in_specs=[SMEM, VMEM, VMEM, VMEM],
        out_specs=[VMEM, VMEM],
        scratch_shapes=[pltpu.VMEM((blocks, pairs * SUB, BW), jnp.float32)],
        compiler_params=PARAMS,
        cost_estimate=cost,
        name="gram_bands",
    )(order, other, mine_shifted, own)
    summed = sum_over_rows(bands)
    passed = lax.ppermute(summed, "pairs", swap)
    return pl.pallas_call(
        turn_kernel,
        out_shape=jax.ShapeDtypeStruct((rows, width), jnp.float32),
        in_specs=[HBM] + [VMEM] * 5,
        out_specs=HBM,
        scratch_shapes=[
            pltpu.VMEM((held, rows, BW), jnp.float32),
            pltpu.VMEM((2, len(FACTORS), pairs, BW), jnp.float32),
            pltpu.SMEM(plan.shape, plan.dtype),
            pltpu.SemaphoreType.DMA((held,)),
            pltpu.SemaphoreType.DMA,
        ],
        compiler_params=PARAMS,
        name="turn_columns",
    )(order, summed, passed, other, mine_shifted, other_shifted)


def solution(mesh):
    return jax.shard_map(
        body,
        mesh=mesh,
        in_specs=(P(("groups", "rows"), "pairs"), P()),
        out_specs=P(("groups", "rows"), "pairs"),
        check_vma=False,
    )
```

```python
import functools

import jax
import jax.numpy as jnp
from jax import lax
from jax.experimental import pallas as pl
from jax.experimental.pallas import tpu as pltpu
from jax.sharding import PartitionSpec as P

BW = 128
STEPS = 4
SUB = 8
BANDS = (
    [("uu", d) for d in range(STEPS)]
    + [("ll", d) for d in range(STEPS)]
    + [("ul", d) for d in range(STEPS)]
    + [("lu", d) for d in range(1, STEPS)]
)
SMEM = pl.BlockSpec(memory_space=pltpu.SMEM)
VMEM = pl.BlockSpec(memory_space=pltpu.VMEM)
BAND_ROWS = 16
HBM = pl.BlockSpec(memory_space=pl.ANY)
PARAMS = pltpu.CompilerParams(vmem_limit_bytes=24 * 1024 * 1024)


def ahead(values, d):
    return values if d == 0 else pltpu.roll(values, BW - d, 1)


def columns_of(slot):
    return pl.ds(pl.multiple_of(slot * BW, BW), BW)


def core_of(block, held):
    return lax.div(block, jnp.int32(held))


def slot_of(block, held):
    return lax.rem(block, jnp.int32(held))


def add(total, term):
    return term if total is None else total + term


def share_pairs(plan, order, held):
    pairs = plan.shape[1] // 2

    straddling, taken = jnp.int32(0), jnp.int32(0)
    for pair in range(pairs):
        first, second = plan[0, 2 * pair], plan[0, 2 * pair + 1]
        inside = core_of(first, held) == core_of(second, held)
        core = jnp.where(inside, core_of(first, held), straddling & 1)
        place = jnp.where(core == 0, taken, pairs // 2 + pair - taken)
        order[0, 2 * place] = first
        order[0, 2 * place + 1] = second
        straddling += jnp.where(inside, 0, 1)
        taken += 1 - core


def shift_kernel(plan, matrix, order, shifted, own, plan_here, order_here, sem, plan_sem, order_sem):
    rows = matrix.shape[0]
    held = matrix.shape[1] // BW

    def fetch(slot):
        columns = columns_of(slot)
        return pltpu.make_async_copy(matrix.at[:, columns], shifted.at[0, :, columns], sem.at[slot])

    for slot in range(held):
        fetch(slot).start()
    plan_copy = pltpu.make_async_copy(plan, plan_here, plan_sem)
    plan_copy.start()

    def one(slot, carry):
        fetch(slot).wait()
        columns = columns_of(slot)
        sums = [None] * STEPS
        for row in range(0, rows, SUB):
            here = shifted[0, pl.ds(row, SUB), columns]
            for d in range(STEPS):
                moved = ahead(here, d)
                sums[d] = add(sums[d], here * moved)
                if d:
                    shifted[d, pl.ds(row, SUB), columns] = moved
        for d in range(STEPS):
            own[slot, d] = sums[d]
        return carry

    lax.fori_loop(0, held // 2, one, 0)
    plan_copy.wait()
    share_pairs(plan_here, order_here, held)
    order_copy = pltpu.make_async_copy(order_here, order, order_sem)
    order_copy.start()
    lax.fori_loop(held // 2, held, one, 0)
    order_copy.wait()


def gram_kernel(order, other, mine_shifted, own, bands, other_shifted, partial):
    rows, width = other.shape
    held = width // BW
    pairs = order.shape[1] // 4
    me = lax.axis_index("pairs")

    def one_pair(pair, carry):
        first, second = order[0, 2 * (me * pairs + pair)], order[0, 2 * (me * pairs + pair) + 1]
        first_mine, second_mine = core_of(first, held) == me, core_of(second, held) == me

        def go(u_here, l_here):
            def load(here, slot, row):
                at = pl.ds(row, SUB), columns_of(slot)
                if here:
                    return [mine_shifted[(d, *at)] for d in range(STEPS)]
                values = other[at]
                moved = [ahead(values, d) for d in range(STEPS)]
                for d in range(1, STEPS):
                    other_shifted[(d - 1, *at)] = moved[d]
                return moved

            u_slot, l_slot = slot_of(first, held), slot_of(second, held)
            sums = {}
            for row in range(0, rows, SUB):
                u, l = load(u_here, u_slot, row), load(l_here, l_slot, row)
                for kind, d in BANDS:
                    if (kind == "uu" and u_here) or (kind == "ll" and l_here):
                        continue
                    term = (u if kind[0] == "u" else l)[0] * (u if kind[1] == "u" else l)[d]
                    sums[kind, d] = add(sums.get((kind, d)), term)
            for d in range(STEPS):
                if u_here:
                    sums["uu", d] = own[u_slot, d]
                if l_here:
                    sums["ll", d] = own[l_slot, d]
            for n, key in enumerate(BANDS):
                at = pl.multiple_of((n * pairs + pair) * SUB, SUB)
                partial[pl.ds(at, SUB), :] = sums[key]

        for u_here, l_here in ((True, True), (True, False), (False, True)):
            pl.when((first_mine == u_here) & (second_mine == l_here))(
                functools.partial(go, u_here, l_here)
            )
        return carry

    lax.fori_loop(0, pairs, one_pair, 0)
    used = len(BANDS) * pairs
    partial[pl.ds(used * SUB, (BAND_ROWS * pairs - used) * SUB), :] = jnp.zeros(
        ((BAND_ROWS * pairs - used) * SUB, BW), jnp.float32
    )
    for row in range(0, BAND_ROWS * pairs, SUB):
        total = None
        for sub in range(SUB):
            total = add(total, partial[pl.ds(row * SUB + sub, SUB, stride=SUB), :])
        bands[pl.ds(row, SUB), :] = total


def shift_rest_kernel(order, bands, other, kept, other_shifted):
    held = other.shape[1] // BW
    pairs = order.shape[1] // 4
    me = lax.axis_index("pairs")
    kept[...] = bands[...]

    def one(i, carry):
        block = order[0, 2 * (1 - me) * pairs + i]
        partner = order[0, 2 * (1 - me) * pairs + i + 1 - 2 * (i & 1)]

        @pl.when((core_of(block, held) != me) & (core_of(partner, held) == me))
        def _():
            columns = columns_of(slot_of(block, held))
            for row in range(0, other.shape[0], SUB):
                here = other[pl.ds(row, SUB), columns]
                for d in range(1, STEPS):
                    other_shifted[d - 1, pl.ds(row, SUB), columns] = ahead(here, d)

        return carry

    lax.fori_loop(0, 2 * pairs, one, 0)


def rotation(upper, lower, cross):
    spread = lower - upper
    twice = jnp.where(spread >= 0, 2.0 * cross, -2.0 * cross)
    spread = jnp.abs(spread)
    scale = jnp.maximum(spread, jnp.abs(twice))
    zero = scale == 0
    scale = jnp.where(zero, 1.0, scale)
    x = jnp.where(zero, 1.0, spread / scale)
    y = twice / scale
    length = jnp.sqrt(x * x + y * y)
    cos_v = jnp.sqrt(0.5 + 0.5 * (x / length))
    sin_v = y / (2.0 * length * cos_v)
    return cos_v, sin_v


def jacobi_bands(g):
    turns = []
    for step in range(STEPS):
        cos_v, sin_v = rotation(g["uu", 0], g["ll", 0], g["ul", 0])
        turns.append((cos_v, sin_v))
        left = STEPS - 1 - step
        if left == 0:
            break
        new = {}
        for d in range(left + 1):
            cos_d, sin_d = ahead(cos_v, d), ahead(sin_v, d)
            uu, ll, ul = g["uu", d], g["ll", d], g["ul", d]
            lu = g["lu", d] if d else ul
            a, b = cos_v * uu - sin_v * lu, cos_v * ul - sin_v * ll
            e, f = sin_v * uu + cos_v * lu, sin_v * ul + cos_v * ll
            new["uu", d] = cos_d * a - sin_d * b
            new["ul", d] = sin_d * a + cos_d * b
            new["lu", d] = cos_d * e - sin_d * f
            new["ll", d] = sin_d * e + cos_d * f
        g = {}
        for d in range(left):
            g["uu", d] = new["uu", d]
            g["ll", d] = ahead(new["ll", d], 1)
            g["ul", d] = new["ul", d + 1]
            if d:
                g["lu", d] = ahead(new["ul", 0] if d == 1 else new["lu", d - 1], 1)
    return turns


def basis_bands(turns):
    x, y = {("u", 0): 1.0}, {("l", 0): 1.0}
    for step, (cos_v, sin_v) in enumerate(turns):
        if step:
            y = {(kind, i + 1): ahead(value, 1) for (kind, i), value in y.items()}
        keys = sorted(set(x) | set(y))
        new_x, new_y = {}, {}
        for key in keys:
            if key not in y:
                new_x[key], new_y[key] = cos_v * x[key], sin_v * x[key]
            elif key not in x:
                new_x[key], new_y[key] = -sin_v * y[key], cos_v * y[key]
            else:
                new_x[key] = cos_v * x[key] - sin_v * y[key]
                new_y[key] = sin_v * x[key] + cos_v * y[key]
        x, y = new_x, new_y
    return x, y


FACTORS = [(kind, i) for kind in "ul" for i in range(STEPS)]


def turn_kernel(
    order_there,
    summed,
    passed,
    other,
    mine_shifted,
    own_half,
    other_half,
    out,
    turned,
    bands,
    factors,
    order,
    sem,
    order_sem,
):
    rows, width = other.shape
    held = width // BW
    pairs = order.shape[1] // 4
    me = lax.axis_index("pairs")
    order_copy = pltpu.make_async_copy(order_there, order, order_sem)
    order_copy.start()
    for n in range(len(BANDS)):
        mine, theirs = summed[pl.ds(n * pairs, pairs), :], passed[pl.ds(n * pairs, pairs), :]
        bands[n, pl.ds(0, pairs), :] = jnp.where(me == 0, mine, theirs)
        bands[n, pl.ds(pairs, pairs), :] = jnp.where(me == 0, theirs, mine)
    x, y = basis_bands(jacobi_bands({key: bands[n] for n, key in enumerate(BANDS)}))
    for n, key in enumerate(FACTORS):
        factors[0, n] = x[key]
        factors[1, n] = y[key]
    order_copy.wait()

    def send(slot):
        return pltpu.make_async_copy(turned.at[slot], out.at[:, columns_of(slot)], sem.at[slot])

    def one_pair(other_shifted, cases, base, i, carry):
        pair = base + i
        first, second = order[0, 2 * pair], order[0, 2 * pair + 1]
        first_mine, second_mine = core_of(first, held) == me, core_of(second, held) == me

        def go(u_here, l_here):
            slots = {"u": slot_of(first, held), "l": slot_of(second, held)}
            here = {"u": u_here, "l": l_here}
            scale = [
                [jnp.broadcast_to(factors[side, n, pl.ds(pair, 1), :], (SUB, BW)) for n in range(len(FACTORS))]
                for side in range(2)
            ]
            for row in range(0, rows, SUB):
                total = [None, None]
                for n, (kind, i) in enumerate(FACTORS):
                    at = pl.ds(row, SUB), columns_of(slots[kind])
                    if here[kind]:
                        value = mine_shifted[(i, *at)]
                    else:
                        value = other_shifted[(i - 1, *at)] if i else other[at]
                    for side, kept in enumerate((u_here, l_here)):
                        if kept:
                            total[side] = add(total[side], scale[side][n] * value)
                if u_here:
                    turned[slots["u"], pl.ds(row, SUB), :] = total[0]
                if l_here:
                    turned[slots["l"], pl.ds(row, SUB), :] = ahead(total[1], BW - (STEPS - 1))
            for kind in "ul":
                if here[kind]:
                    send(slots[kind]).start()

        for u_here, l_here in cases:
            pl.when((first_mine == u_here) & (second_mine == l_here))(
                functools.partial(go, u_here, l_here)
            )
        return carry

    straddling = ((True, False), (False, True))
    lax.fori_loop(0, pairs, functools.partial(one_pair, own_half, ((True, True), *straddling), me * pairs), 0)
    lax.fori_loop(0, pairs, functools.partial(one_pair, other_half, straddling, (1 - me) * pairs), 0)
    for slot in range(held):
        send(slot).wait()


def sum_over_rows(values, first):
    size = lax.axis_size("rows")
    if size & (size - 1):
        return lax.psum(values, "rows")
    got = [
        lax.ppermute(values, "rows", [(i, i ^ m) for i in range(size)]) for m in (1, 2, 3) if m < size
    ]
    summed = first
    if got:
        summed = summed + got[0]
    if got[1:]:
        summed = summed + (got[1] + got[2])
    stride = 4
    while stride < size:
        summed = summed + lax.ppermute(summed, "rows", [(i, i ^ stride) for i in range(size)])
        stride *= 2
    return summed


def body(matrix, plan):
    rows, width = matrix.shape
    held = width // BW
    pairs = held // 2
    swap = [(0, 1), (1, 0)]
    other = lax.ppermute(matrix, "pairs", swap)
    cost = pl.CostEstimate(flops=30 * rows * width, bytes_accessed=8 * rows * width, transcendentals=0)
    columns = jax.ShapeDtypeStruct((STEPS - 1, rows, width), jnp.float32)
    bands_shape = jax.ShapeDtypeStruct((BAND_ROWS * pairs, BW), jnp.float32)
    order, mine_shifted, own = pl.pallas_call(
        shift_kernel,
        out_shape=[
            jax.ShapeDtypeStruct(plan.shape, plan.dtype),
            jax.ShapeDtypeStruct((STEPS, rows, width), jnp.float32),
            jax.ShapeDtypeStruct((held, STEPS, SUB, BW), jnp.float32),
        ],
        in_specs=[HBM, HBM],
        out_specs=[HBM, VMEM, VMEM],
        scratch_shapes=[
            pltpu.SMEM(plan.shape, plan.dtype),
            pltpu.SMEM(plan.shape, plan.dtype),
            pltpu.SemaphoreType.DMA((held,)),
            pltpu.SemaphoreType.DMA,
            pltpu.SemaphoreType.DMA,
        ],
        compiler_params=PARAMS,
        cost_estimate=cost,
        name="shift_own",
    )(
        pltpu.with_memory_space_constraint(plan, pltpu.HBM),
        pltpu.with_memory_space_constraint(matrix, pltpu.HBM),
    )
    bands, own_half = pl.pallas_call(
        gram_kernel,
        out_shape=[bands_shape, columns],
        in_specs=[SMEM, VMEM, VMEM, VMEM],
        out_specs=[VMEM, VMEM],
        scratch_shapes=[pltpu.VMEM((BAND_ROWS * pairs * SUB, BW), jnp.float32)],
        compiler_params=PARAMS,
        cost_estimate=cost,
        name="gram_bands",
    )(order, other, mine_shifted, own)
    kept, other_half = pl.pallas_call(
        shift_rest_kernel,
        out_shape=[bands_shape, columns],
        in_specs=[SMEM, VMEM, VMEM],
        out_specs=[VMEM, VMEM],
        compiler_params=PARAMS,
        cost_estimate=cost,
        name="shift_rest",
    )(order, bands, other)
    summed = sum_over_rows(bands, kept)
    passed = lax.ppermute(summed, "pairs", swap)
    return pl.pallas_call(
        turn_kernel,
        out_shape=jax.ShapeDtypeStruct((rows, width), jnp.float32),
        in_specs=[HBM] + [VMEM] * 6,
        out_specs=HBM,
        scratch_shapes=[
            pltpu.VMEM((held, rows, BW), jnp.float32),
            pltpu.VMEM((len(BANDS), 2 * pairs, BW), jnp.float32),
            pltpu.VMEM((2, len(FACTORS), 2 * pairs, BW), jnp.float32),
            pltpu.SMEM(plan.shape, plan.dtype),
            pltpu.SemaphoreType.DMA((held,)),
            pltpu.SemaphoreType.DMA,
        ],
        compiler_params=PARAMS,
        name="turn_columns",
    )(order, summed, passed, other, mine_shifted, own_half, other_half)


def solution(mesh):
    return jax.shard_map(
        body,
        mesh=mesh,
        in_specs=(P(("groups", "rows"), "pairs"), P()),
        out_specs=P(("groups", "rows"), "pairs"),
        check_vma=False,
    )
```

```python
import functools

import jax
import jax.numpy as jnp
from jax import lax
from jax.experimental import pallas as pl
from jax.experimental.pallas import tpu as pltpu
from jax.sharding import PartitionSpec as P

BW = 128
STEPS = 4
SUB = 8
BANDS = (
    [("uu", d) for d in range(STEPS)]
    + [("ll", d) for d in range(STEPS)]
    + [("ul", d) for d in range(STEPS)]
    + [("lu", d) for d in range(1, STEPS)]
)
SMEM = pl.BlockSpec(memory_space=pltpu.SMEM)
VMEM = pl.BlockSpec(memory_space=pltpu.VMEM)
BAND_ROWS = 16
HBM = pl.BlockSpec(memory_space=pl.ANY)
PARAMS = pltpu.CompilerParams(vmem_limit_bytes=24 * 1024 * 1024)


def ahead(values, d):
    return values if d == 0 else pltpu.roll(values, BW - d, 1)


def columns_of(slot):
    return pl.ds(pl.multiple_of(slot * BW, BW), BW)


def core_of(block, held):
    return lax.div(block, jnp.int32(held))


def slot_of(block, held):
    return lax.rem(block, jnp.int32(held))


def add(total, term):
    return term if total is None else total + term


def parity(row):
    for shift in (8, 4, 2, 1):
        row = row ^ (row >> shift)
    return row & 1


def half_here():
    return lax.axis_index("pairs") ^ parity(lax.axis_index("rows"))


def share_pairs(plan, order, held):
    pairs = plan.shape[1] // 2
    seen = [jnp.int32(0)] * 3
    taken = jnp.int32(0)
    for pair in range(pairs):
        first, second = plan[0, 2 * pair], plan[0, 2 * pair + 1]
        core = core_of(first, held)
        kind = jnp.where(core == core_of(second, held), core, 2)
        count = jnp.where(kind == 2, seen[2], jnp.where(kind == 1, seen[1] + 1, seen[0]))
        half = count & 1
        place = jnp.where(half == 0, taken, pairs // 2 + pair - taken)
        order[0, 2 * place] = first
        order[0, 2 * place + 1] = second
        taken += 1 - half
        seen = [n + jnp.where(kind == k, 1, 0) for k, n in enumerate(seen)]


def shift_kernel(plan, matrix, order, shifted, own, plan_here, order_here, sem, plan_sem, order_sem):
    rows = matrix.shape[0]
    held = matrix.shape[1] // BW

    def fetch(slot):
        columns = columns_of(slot)
        return pltpu.make_async_copy(matrix.at[:, columns], shifted.at[0, :, columns], sem.at[slot])

    for slot in range(held):
        fetch(slot).start()
    plan_copy = pltpu.make_async_copy(plan, plan_here, plan_sem)
    plan_copy.start()

    def one(slot, carry):
        fetch(slot).wait()
        columns = columns_of(slot)
        sums = [None] * STEPS
        for row in range(0, rows, SUB):
            here = shifted[0, pl.ds(row, SUB), columns]
            for d in range(STEPS):
                moved = ahead(here, d)
                sums[d] = add(sums[d], here * moved)
                if d:
                    shifted[d, pl.ds(row, SUB), columns] = moved
        for d in range(STEPS):
            own[slot, d] = sums[d]
        return carry

    lax.fori_loop(0, held // 2, one, 0)
    plan_copy.wait()
    share_pairs(plan_here, order_here, held)
    order_copy = pltpu.make_async_copy(order_here, order, order_sem)
    order_copy.start()
    lax.fori_loop(held // 2, held, one, 0)
    order_copy.wait()


def gram_kernel(order, other, mine_shifted, own, bands, other_shifted, partial):
    rows, width = other.shape
    held = width // BW
    pairs = order.shape[1] // 4
    me = lax.axis_index("pairs")
    base = half_here() * pairs

    def one_pair(pair, carry):
        first, second = order[0, 2 * (base + pair)], order[0, 2 * (base + pair) + 1]
        first_mine, second_mine = core_of(first, held) == me, core_of(second, held) == me

        def go(u_here, l_here):
            def load(here, slot, row):
                at = pl.ds(row, SUB), columns_of(slot)
                if here:
                    return [mine_shifted[(d, *at)] for d in range(STEPS)]
                values = other[at]
                moved = [ahead(values, d) for d in range(STEPS)]
                if u_here or l_here:
                    for d in range(1, STEPS):
                        other_shifted[(d - 1, *at)] = moved[d]
                return moved

            u_slot, l_slot = slot_of(first, held), slot_of(second, held)
            sums = {}
            for row in range(0, rows, SUB):
                u, l = load(u_here, u_slot, row), load(l_here, l_slot, row)
                for kind, d in BANDS:
                    if (kind == "uu" and u_here) or (kind == "ll" and l_here):
                        continue
                    term = (u if kind[0] == "u" else l)[0] * (u if kind[1] == "u" else l)[d]
                    sums[kind, d] = add(sums.get((kind, d)), term)
            for d in range(STEPS):
                if u_here:
                    sums["uu", d] = own[u_slot, d]
                if l_here:
                    sums["ll", d] = own[l_slot, d]
            for n, key in enumerate(BANDS):
                at = pl.multiple_of((n * pairs + pair) * SUB, SUB)
                partial[pl.ds(at, SUB), :] = sums[key]

        for u_here, l_here in ((True, True), (True, False), (False, True), (False, False)):
            pl.when((first_mine == u_here) & (second_mine == l_here))(
                functools.partial(go, u_here, l_here)
            )
        return carry

    lax.fori_loop(0, pairs, one_pair, 0)
    used = len(BANDS) * pairs
    partial[pl.ds(used * SUB, (BAND_ROWS * pairs - used) * SUB), :] = jnp.zeros(
        ((BAND_ROWS * pairs - used) * SUB, BW), jnp.float32
    )
    for row in range(0, BAND_ROWS * pairs, SUB):
        total = None
        for sub in range(SUB):
            total = add(total, partial[pl.ds(row * SUB + sub, SUB, stride=SUB), :])
        bands[pl.ds(row, SUB), :] = total


def shift_rest_kernel(order, bands, other, kept, other_shifted):
    held = other.shape[1] // BW
    pairs = order.shape[1] // 4
    me = lax.axis_index("pairs")
    base = 2 * (1 - half_here()) * pairs
    kept[...] = bands[...]

    def one(i, carry):
        block = order[0, base + i]
        partner = order[0, base + i + 1 - 2 * (i & 1)]

        @pl.when((core_of(block, held) != me) & (core_of(partner, held) == me))
        def _():
            columns = columns_of(slot_of(block, held))
            for row in range(0, other.shape[0], SUB):
                here = other[pl.ds(row, SUB), columns]
                for d in range(1, STEPS):
                    other_shifted[d - 1, pl.ds(row, SUB), columns] = ahead(here, d)

        return carry

    lax.fori_loop(0, 2 * pairs, one, 0)


def rotation(upper, lower, cross):
    spread = lower - upper
    twice = jnp.where(spread >= 0, 2.0 * cross, -2.0 * cross)
    spread = jnp.abs(spread)
    scale = jnp.maximum(spread, jnp.abs(twice))
    zero = scale == 0
    scale = jnp.where(zero, 1.0, scale)
    x = jnp.where(zero, 1.0, spread / scale)
    y = twice / scale
    length = jnp.sqrt(x * x + y * y)
    cos_v = jnp.sqrt(0.5 + 0.5 * (x / length))
    sin_v = y / (2.0 * length * cos_v)
    return cos_v, sin_v


def jacobi_bands(g):
    turns = []
    for step in range(STEPS):
        cos_v, sin_v = rotation(g["uu", 0], g["ll", 0], g["ul", 0])
        turns.append((cos_v, sin_v))
        left = STEPS - 1 - step
        if left == 0:
            break
        new = {}
        for d in range(left + 1):
            cos_d, sin_d = ahead(cos_v, d), ahead(sin_v, d)
            uu, ll, ul = g["uu", d], g["ll", d], g["ul", d]
            lu = g["lu", d] if d else ul
            a, b = cos_v * uu - sin_v * lu, cos_v * ul - sin_v * ll
            e, f = sin_v * uu + cos_v * lu, sin_v * ul + cos_v * ll
            new["uu", d] = cos_d * a - sin_d * b
            new["ul", d] = sin_d * a + cos_d * b
            new["lu", d] = cos_d * e - sin_d * f
            new["ll", d] = sin_d * e + cos_d * f
        g = {}
        for d in range(left):
            g["uu", d] = new["uu", d]
            g["ll", d] = ahead(new["ll", d], 1)
            g["ul", d] = new["ul", d + 1]
            if d:
                g["lu", d] = ahead(new["ul", 0] if d == 1 else new["lu", d - 1], 1)
    return turns


def basis_bands(turns):
    x, y = {("u", 0): 1.0}, {("l", 0): 1.0}
    for step, (cos_v, sin_v) in enumerate(turns):
        if step:
            y = {(kind, i + 1): ahead(value, 1) for (kind, i), value in y.items()}
        keys = sorted(set(x) | set(y))
        new_x, new_y = {}, {}
        for key in keys:
            if key not in y:
                new_x[key], new_y[key] = cos_v * x[key], sin_v * x[key]
            elif key not in x:
                new_x[key], new_y[key] = -sin_v * y[key], cos_v * y[key]
            else:
                new_x[key] = cos_v * x[key] - sin_v * y[key]
                new_y[key] = sin_v * x[key] + cos_v * y[key]
        x, y = new_x, new_y
    return x, y


FACTORS = [(kind, i) for kind in "ul" for i in range(STEPS)]


def turn_kernel(
    order_there,
    summed,
    passed,
    other,
    mine_shifted,
    own_half,
    other_half,
    out,
    turned,
    bands,
    factors,
    order,
    sem,
    order_sem,
):
    rows, width = other.shape
    held = width // BW
    pairs = order.shape[1] // 4
    me = lax.axis_index("pairs")
    half = half_here()
    order_copy = pltpu.make_async_copy(order_there, order, order_sem)
    order_copy.start()
    for n in range(len(BANDS)):
        mine, theirs = summed[pl.ds(n * pairs, pairs), :], passed[pl.ds(n * pairs, pairs), :]
        bands[n, pl.ds(0, pairs), :] = jnp.where(half == 0, mine, theirs)
        bands[n, pl.ds(pairs, pairs), :] = jnp.where(half == 0, theirs, mine)
    x, y = basis_bands(jacobi_bands({key: bands[n] for n, key in enumerate(BANDS)}))
    for n, key in enumerate(FACTORS):
        factors[0, n] = x[key]
        factors[1, n] = y[key]
    order_copy.wait()

    def send(slot):
        return pltpu.make_async_copy(turned.at[slot], out.at[:, columns_of(slot)], sem.at[slot])

    def one_pair(other_shifted, base, i, carry):
        pair = base + i
        first, second = order[0, 2 * pair], order[0, 2 * pair + 1]
        first_mine, second_mine = core_of(first, held) == me, core_of(second, held) == me

        def go(u_here, l_here):
            slots = {"u": slot_of(first, held), "l": slot_of(second, held)}
            here = {"u": u_here, "l": l_here}
            scale = [
                [jnp.broadcast_to(factors[side, n, pl.ds(pair, 1), :], (SUB, BW)) for n in range(len(FACTORS))]
                for side in range(2)
            ]
            for row in range(0, rows, SUB):
                total = [None, None]
                for n, (kind, i) in enumerate(FACTORS):
                    at = pl.ds(row, SUB), columns_of(slots[kind])
                    if here[kind]:
                        value = mine_shifted[(i, *at)]
                    else:
                        value = other_shifted[(i - 1, *at)] if i else other[at]
                    for side, kept in enumerate((u_here, l_here)):
                        if kept:
                            total[side] = add(total[side], scale[side][n] * value)
                if u_here:
                    turned[slots["u"], pl.ds(row, SUB), :] = total[0]
                if l_here:
                    turned[slots["l"], pl.ds(row, SUB), :] = ahead(total[1], BW - (STEPS - 1))
            for kind in "ul":
                if here[kind]:
                    send(slots[kind]).start()

        for u_here, l_here in ((True, True), (True, False), (False, True)):
            pl.when((first_mine == u_here) & (second_mine == l_here))(
                functools.partial(go, u_here, l_here)
            )
        return carry

    lax.fori_loop(0, pairs, functools.partial(one_pair, own_half, half * pairs), 0)
    lax.fori_loop(0, pairs, functools.partial(one_pair, other_half, (1 - half) * pairs), 0)
    for slot in range(held):
        send(slot).wait()


def exchange(values, step):
    size, cores = lax.axis_size("rows"), lax.axis_size("pairs")
    route = [
        (row * cores + core, (row ^ step) * cores + (core ^ parity(step)))
        for row in range(size)
        for core in range(cores)
    ]
    return lax.ppermute(values, ("rows", "pairs"), route)


def sum_over_rows(values, later):
    size = lax.axis_size("rows")
    if size & (size - 1):
        raise ValueError("rows")
    got = [exchange(values, step) for step in (1, 2, 3) if step < size]
    summed = later
    if got:
        summed = summed + got[0]
    if got[1:]:
        summed = summed + (got[1] + got[2])
    stride = 4
    while stride < size:
        summed = summed + exchange(summed, stride)
        stride *= 2
    return summed


def body(matrix, plan):
    rows, width = matrix.shape
    held = width // BW
    pairs = held // 2
    swap = [(0, 1), (1, 0)]
    other = lax.ppermute(matrix, "pairs", swap)
    cost = pl.CostEstimate(flops=30 * rows * width, bytes_accessed=8 * rows * width, transcendentals=0)
    columns = jax.ShapeDtypeStruct((STEPS - 1, rows, width), jnp.float32)
    bands_shape = jax.ShapeDtypeStruct((BAND_ROWS * pairs, BW), jnp.float32)
    order, mine_shifted, own = pl.pallas_call(
        shift_kernel,
        out_shape=[
            jax.ShapeDtypeStruct(plan.shape, plan.dtype),
            jax.ShapeDtypeStruct((STEPS, rows, width), jnp.float32),
            jax.ShapeDtypeStruct((held, STEPS, SUB, BW), jnp.float32),
        ],
        in_specs=[HBM, HBM],
        out_specs=[HBM, VMEM, VMEM],
        scratch_shapes=[
            pltpu.SMEM(plan.shape, plan.dtype),
            pltpu.SMEM(plan.shape, plan.dtype),
            pltpu.SemaphoreType.DMA((held,)),
            pltpu.SemaphoreType.DMA,
            pltpu.SemaphoreType.DMA,
        ],
        compiler_params=PARAMS,
        cost_estimate=cost,
        name="shift_own",
    )(
        pltpu.with_memory_space_constraint(plan, pltpu.HBM),
        pltpu.with_memory_space_constraint(matrix, pltpu.HBM),
    )
    bands, own_half = pl.pallas_call(
        gram_kernel,
        out_shape=[bands_shape, columns],
        in_specs=[SMEM, VMEM, VMEM, VMEM],
        out_specs=[VMEM, VMEM],
        scratch_shapes=[pltpu.VMEM((BAND_ROWS * pairs * SUB, BW), jnp.float32)],
        compiler_params=PARAMS,
        cost_estimate=cost,
        name="gram_bands",
    )(order, other, mine_shifted, own)
    kept, other_half = pl.pallas_call(
        shift_rest_kernel,
        out_shape=[bands_shape, columns],
        in_specs=[SMEM, VMEM, VMEM],
        out_specs=[VMEM, VMEM],
        compiler_params=PARAMS,
        cost_estimate=cost,
        name="shift_rest",
    )(order, bands, other)
    summed = sum_over_rows(bands, kept)
    passed = lax.ppermute(summed, "pairs", swap)
    return pl.pallas_call(
        turn_kernel,
        out_shape=jax.ShapeDtypeStruct((rows, width), jnp.float32),
        in_specs=[HBM] + [VMEM] * 6,
        out_specs=HBM,
        scratch_shapes=[
            pltpu.VMEM((held, rows, BW), jnp.float32),
            pltpu.VMEM((len(BANDS), 2 * pairs, BW), jnp.float32),
            pltpu.VMEM((2, len(FACTORS), 2 * pairs, BW), jnp.float32),
            pltpu.SMEM(plan.shape, plan.dtype),
            pltpu.SemaphoreType.DMA((held,)),
            pltpu.SemaphoreType.DMA,
        ],
        compiler_params=PARAMS,
        name="turn_columns",
    )(order, summed, passed, other, mine_shifted, own_half, other_half)


def solution(mesh):
    return jax.shard_map(
        body,
        mesh=mesh,
        in_specs=(P(("groups", "rows"), "pairs"), P()),
        out_specs=P(("groups", "rows"), "pairs"),
        check_vma=False,
    )
```

```python
import functools

import jax
import jax.numpy as jnp
from jax import lax
from jax.experimental import pallas as pl
from jax.experimental.pallas import tpu as pltpu
from jax.sharding import PartitionSpec as P

BW = 128
STEPS = 4
SUB = 8
BANDS = (
    [("uu", d) for d in range(STEPS)]
    + [("ll", d) for d in range(STEPS)]
    + [("ul", d) for d in range(STEPS)]
    + [("lu", d) for d in range(1, STEPS)]
)
SMEM = pl.BlockSpec(memory_space=pltpu.SMEM)
VMEM = pl.BlockSpec(memory_space=pltpu.VMEM)
BAND_ROWS = 16
CHUNK = 64
HBM = pl.BlockSpec(memory_space=pl.ANY)
PARAMS = pltpu.CompilerParams(vmem_limit_bytes=24 * 1024 * 1024)


def ahead(values, d):
    return values if d == 0 else pltpu.roll(values, BW - d, 1)


def columns_of(slot):
    return pl.ds(pl.multiple_of(slot * BW, BW), BW)


def core_of(block, held):
    return lax.div(block, jnp.int32(held))


def slot_of(block, held):
    return lax.rem(block, jnp.int32(held))


def over_rows(rows, step, carry):
    def chunk(i, carry):
        for row in range(0, CHUNK, SUB):
            carry = step(pl.multiple_of(i * CHUNK + row, SUB), carry)
        return carry

    return lax.fori_loop(0, rows // CHUNK, chunk, carry)


def add(total, term):
    return term if total is None else total + term


def parity(row):
    for shift in (8, 4, 2, 1):
        row = row ^ (row >> shift)
    return row & 1


def half_here():
    return lax.axis_index("pairs") ^ parity(lax.axis_index("rows"))


def share_pairs(plan, order, held):
    pairs = plan.shape[1] // 2
    seen = [jnp.int32(0)] * 3
    taken = jnp.int32(0)
    for pair in range(pairs):
        first, second = plan[0, 2 * pair], plan[0, 2 * pair + 1]
        core = core_of(first, held)
        kind = jnp.where(core == core_of(second, held), core, 2)
        count = jnp.where(kind == 2, seen[2], jnp.where(kind == 1, seen[1] + 1, seen[0]))
        half = count & 1
        place = jnp.where(half == 0, taken, pairs // 2 + pair - taken)
        order[0, 2 * place] = first
        order[0, 2 * place + 1] = second
        taken += 1 - half
        seen = [n + jnp.where(kind == k, 1, 0) for k, n in enumerate(seen)]


def shift_kernel(plan, matrix, order, shifted, own, plan_here, order_here, sem, plan_sem, order_sem):
    rows = matrix.shape[0]
    held = matrix.shape[1] // BW

    def fetch(slot):
        columns = columns_of(slot)
        return pltpu.make_async_copy(matrix.at[:, columns], shifted.at[0, :, columns], sem.at[slot])

    for slot in range(held):
        fetch(slot).start()
    plan_copy = pltpu.make_async_copy(plan, plan_here, plan_sem)
    plan_copy.start()

    def one(slot, carry):
        fetch(slot).wait()
        columns = columns_of(slot)

        def step(row, sums):
            here = shifted[0, pl.ds(row, SUB), columns]
            new = []
            for d in range(STEPS):
                moved = ahead(here, d)
                new.append(sums[d] + here * moved)
                if d:
                    shifted[d, pl.ds(row, SUB), columns] = moved
            return tuple(new)

        sums = over_rows(rows, step, (jnp.zeros((SUB, BW), jnp.float32),) * STEPS)
        for d in range(STEPS):
            own[slot, d] = sums[d]
        return carry

    lax.fori_loop(0, held // 2, one, 0)
    plan_copy.wait()
    share_pairs(plan_here, order_here, held)
    order_copy = pltpu.make_async_copy(order_here, order, order_sem)
    order_copy.start()
    lax.fori_loop(held // 2, held, one, 0)
    order_copy.wait()


def gram_kernel(order, other, mine_shifted, own, bands, other_shifted, partial):
    rows, width = other.shape
    held = width // BW
    pairs = order.shape[1] // 4
    me = lax.axis_index("pairs")
    base = half_here() * pairs

    def one_pair(pair, carry):
        first, second = order[0, 2 * (base + pair)], order[0, 2 * (base + pair) + 1]
        first_mine, second_mine = core_of(first, held) == me, core_of(second, held) == me

        def go(u_here, l_here):
            def load(here, slot, row):
                at = pl.ds(row, SUB), columns_of(slot)
                if here:
                    return [mine_shifted[(d, *at)] for d in range(STEPS)]
                values = other[at]
                moved = [ahead(values, d) for d in range(STEPS)]
                if u_here or l_here:
                    for d in range(1, STEPS):
                        other_shifted[(d - 1, *at)] = moved[d]
                return moved

            u_slot, l_slot = slot_of(first, held), slot_of(second, held)
            wanted = [
                (kind, d)
                for kind, d in BANDS
                if not ((kind == "uu" and u_here) or (kind == "ll" and l_here))
            ]

            def step(row, sums):
                u, l = load(u_here, u_slot, row), load(l_here, l_slot, row)
                new = []
                for (kind, d), total in zip(wanted, sums):
                    new.append(total + (u if kind[0] == "u" else l)[0] * (u if kind[1] == "u" else l)[d])
                return tuple(new)

            sums = over_rows(rows, step, (jnp.zeros((SUB, BW), jnp.float32),) * len(wanted))
            sums = dict(zip(wanted, sums))
            for d in range(STEPS):
                if u_here:
                    sums["uu", d] = own[u_slot, d]
                if l_here:
                    sums["ll", d] = own[l_slot, d]
            for n, key in enumerate(BANDS):
                at = pl.multiple_of((n * pairs + pair) * SUB, SUB)
                partial[pl.ds(at, SUB), :] = sums[key]

        for u_here, l_here in ((True, True), (True, False), (False, True), (False, False)):
            pl.when((first_mine == u_here) & (second_mine == l_here))(
                functools.partial(go, u_here, l_here)
            )
        return carry

    lax.fori_loop(0, pairs, one_pair, 0)
    used = len(BANDS) * pairs
    partial[pl.ds(used * SUB, (BAND_ROWS * pairs - used) * SUB), :] = jnp.zeros(
        ((BAND_ROWS * pairs - used) * SUB, BW), jnp.float32
    )
    for row in range(0, BAND_ROWS * pairs, SUB):
        total = None
        for sub in range(SUB):
            total = add(total, partial[pl.ds(row * SUB + sub, SUB, stride=SUB), :])
        bands[pl.ds(row, SUB), :] = total


def shift_rest_kernel(order, bands, other, kept, other_shifted):
    held = other.shape[1] // BW
    pairs = order.shape[1] // 4
    me = lax.axis_index("pairs")
    base = 2 * (1 - half_here()) * pairs
    kept[...] = bands[...]

    def one(i, carry):
        block = order[0, base + i]
        partner = order[0, base + i + 1 - 2 * (i & 1)]

        @pl.when((core_of(block, held) != me) & (core_of(partner, held) == me))
        def _():
            columns = columns_of(slot_of(block, held))

            def step(row, carry):
                here = other[pl.ds(row, SUB), columns]
                for d in range(1, STEPS):
                    other_shifted[d - 1, pl.ds(row, SUB), columns] = ahead(here, d)
                return carry

            over_rows(other.shape[0], step, 0)

        return carry

    lax.fori_loop(0, 2 * pairs, one, 0)


def rotation(upper, lower, cross):
    spread = lower - upper
    twice = jnp.where(spread >= 0, 2.0 * cross, -2.0 * cross)
    spread = jnp.abs(spread)
    scale = jnp.maximum(spread, jnp.abs(twice))
    zero = scale == 0
    scale = jnp.where(zero, 1.0, scale)
    x = jnp.where(zero, 1.0, spread / scale)
    y = twice / scale
    length = jnp.sqrt(x * x + y * y)
    cos_v = jnp.sqrt(0.5 + 0.5 * (x / length))
    sin_v = y / (2.0 * length * cos_v)
    return cos_v, sin_v


def jacobi_bands(g):
    turns = []
    for step in range(STEPS):
        cos_v, sin_v = rotation(g["uu", 0], g["ll", 0], g["ul", 0])
        turns.append((cos_v, sin_v))
        left = STEPS - 1 - step
        if left == 0:
            break
        new = {}
        for d in range(left + 1):
            cos_d, sin_d = ahead(cos_v, d), ahead(sin_v, d)
            uu, ll, ul = g["uu", d], g["ll", d], g["ul", d]
            lu = g["lu", d] if d else ul
            a, b = cos_v * uu - sin_v * lu, cos_v * ul - sin_v * ll
            e, f = sin_v * uu + cos_v * lu, sin_v * ul + cos_v * ll
            new["uu", d] = cos_d * a - sin_d * b
            new["ul", d] = sin_d * a + cos_d * b
            new["lu", d] = cos_d * e - sin_d * f
            new["ll", d] = sin_d * e + cos_d * f
        g = {}
        for d in range(left):
            g["uu", d] = new["uu", d]
            g["ll", d] = ahead(new["ll", d], 1)
            g["ul", d] = new["ul", d + 1]
            if d:
                g["lu", d] = ahead(new["ul", 0] if d == 1 else new["lu", d - 1], 1)
    return turns


def basis_bands(turns):
    x, y = {("u", 0): 1.0}, {("l", 0): 1.0}
    for step, (cos_v, sin_v) in enumerate(turns):
        if step:
            y = {(kind, i + 1): ahead(value, 1) for (kind, i), value in y.items()}
        keys = sorted(set(x) | set(y))
        new_x, new_y = {}, {}
        for key in keys:
            if key not in y:
                new_x[key], new_y[key] = cos_v * x[key], sin_v * x[key]
            elif key not in x:
                new_x[key], new_y[key] = -sin_v * y[key], cos_v * y[key]
            else:
                new_x[key] = cos_v * x[key] - sin_v * y[key]
                new_y[key] = sin_v * x[key] + cos_v * y[key]
        x, y = new_x, new_y
    return x, y


FACTORS = [(kind, i) for kind in "ul" for i in range(STEPS)]


def turn_kernel(
    order_there,
    summed,
    passed,
    other,
    mine_shifted,
    own_half,
    other_half,
    out,
    turned,
    bands,
    factors,
    order,
    sem,
    order_sem,
):
    rows, width = other.shape
    held = width // BW
    pairs = order.shape[1] // 4
    me = lax.axis_index("pairs")
    half = half_here()
    order_copy = pltpu.make_async_copy(order_there, order, order_sem)
    order_copy.start()
    for n in range(len(BANDS)):
        mine, theirs = summed[pl.ds(n * pairs, pairs), :], passed[pl.ds(n * pairs, pairs), :]
        bands[n, pl.ds(0, pairs), :] = jnp.where(half == 0, mine, theirs)
        bands[n, pl.ds(pairs, pairs), :] = jnp.where(half == 0, theirs, mine)
    x, y = basis_bands(jacobi_bands({key: bands[n] for n, key in enumerate(BANDS)}))
    for n, key in enumerate(FACTORS):
        factors[0, n] = x[key]
        factors[1, n] = y[key]
    order_copy.wait()

    def send(slot):
        return pltpu.make_async_copy(turned.at[slot], out.at[:, columns_of(slot)], sem.at[slot])

    def one_pair(other_shifted, base, i, carry):
        pair = base + i
        first, second = order[0, 2 * pair], order[0, 2 * pair + 1]
        first_mine, second_mine = core_of(first, held) == me, core_of(second, held) == me

        def go(u_here, l_here):
            slots = {"u": slot_of(first, held), "l": slot_of(second, held)}
            here = {"u": u_here, "l": l_here}
            scale = [
                [jnp.broadcast_to(factors[side, n, pl.ds(pair, 1), :], (SUB, BW)) for n in range(len(FACTORS))]
                for side in range(2)
            ]

            def step(row, carry):
                total = [None, None]
                for n, (kind, i) in enumerate(FACTORS):
                    at = pl.ds(row, SUB), columns_of(slots[kind])
                    if here[kind]:
                        value = mine_shifted[(i, *at)]
                    else:
                        value = other_shifted[(i - 1, *at)] if i else other[at]
                    for side, kept in enumerate((u_here, l_here)):
                        if kept:
                            total[side] = add(total[side], scale[side][n] * value)
                if u_here:
                    turned[slots["u"], pl.ds(row, SUB), :] = total[0]
                if l_here:
                    turned[slots["l"], pl.ds(row, SUB), :] = ahead(total[1], BW - (STEPS - 1))
                return carry

            over_rows(rows, step, 0)
            for kind in "ul":
                if here[kind]:
                    send(slots[kind]).start()

        for u_here, l_here in ((True, True), (True, False), (False, True)):
            pl.when((first_mine == u_here) & (second_mine == l_here))(
                functools.partial(go, u_here, l_here)
            )
        return carry

    lax.fori_loop(0, pairs, functools.partial(one_pair, own_half, half * pairs), 0)
    lax.fori_loop(0, pairs, functools.partial(one_pair, other_half, (1 - half) * pairs), 0)
    for slot in range(held):
        send(slot).wait()


def exchange(values, step):
    size, cores = lax.axis_size("rows"), lax.axis_size("pairs")
    route = [
        (row * cores + core, (row ^ step) * cores + (core ^ parity(step)))
        for row in range(size)
        for core in range(cores)
    ]
    return lax.ppermute(values, ("rows", "pairs"), route)


def sum_over_rows(values, later):
    size = lax.axis_size("rows")
    if size & (size - 1):
        raise ValueError("rows")
    got = [exchange(values, step) for step in (1, 2, 3) if step < size]
    summed = later
    if got:
        summed = summed + got[0]
    if got[1:]:
        summed = summed + (got[1] + got[2])
    stride = 4
    while stride < size:
        summed = summed + exchange(summed, stride)
        stride *= 2
    return summed


def body(matrix, plan):
    rows, width = matrix.shape
    held = width // BW
    pairs = held // 2
    swap = [(0, 1), (1, 0)]
    other = lax.ppermute(matrix, "pairs", swap)
    cost = pl.CostEstimate(flops=30 * rows * width, bytes_accessed=8 * rows * width, transcendentals=0)
    columns = jax.ShapeDtypeStruct((STEPS - 1, rows, width), jnp.float32)
    bands_shape = jax.ShapeDtypeStruct((BAND_ROWS * pairs, BW), jnp.float32)
    order, mine_shifted, own = pl.pallas_call(
        shift_kernel,
        out_shape=[
            jax.ShapeDtypeStruct(plan.shape, plan.dtype),
            jax.ShapeDtypeStruct((STEPS, rows, width), jnp.float32),
            jax.ShapeDtypeStruct((held, STEPS, SUB, BW), jnp.float32),
        ],
        in_specs=[HBM, HBM],
        out_specs=[HBM, VMEM, VMEM],
        scratch_shapes=[
            pltpu.SMEM(plan.shape, plan.dtype),
            pltpu.SMEM(plan.shape, plan.dtype),
            pltpu.SemaphoreType.DMA((held,)),
            pltpu.SemaphoreType.DMA,
            pltpu.SemaphoreType.DMA,
        ],
        compiler_params=PARAMS,
        cost_estimate=cost,
        name="shift_own",
    )(
        pltpu.with_memory_space_constraint(plan, pltpu.HBM),
        pltpu.with_memory_space_constraint(matrix, pltpu.HBM),
    )
    bands, own_half = pl.pallas_call(
        gram_kernel,
        out_shape=[bands_shape, columns],
        in_specs=[SMEM, VMEM, VMEM, VMEM],
        out_specs=[VMEM, VMEM],
        scratch_shapes=[pltpu.VMEM((BAND_ROWS * pairs * SUB, BW), jnp.float32)],
        compiler_params=PARAMS,
        cost_estimate=cost,
        name="gram_bands",
    )(order, other, mine_shifted, own)
    kept, other_half = pl.pallas_call(
        shift_rest_kernel,
        out_shape=[bands_shape, columns],
        in_specs=[SMEM, VMEM, VMEM],
        out_specs=[VMEM, VMEM],
        compiler_params=PARAMS,
        cost_estimate=cost,
        name="shift_rest",
    )(order, bands, other)
    summed = sum_over_rows(bands, kept)
    passed = lax.ppermute(summed, "pairs", swap)
    return pl.pallas_call(
        turn_kernel,
        out_shape=jax.ShapeDtypeStruct((rows, width), jnp.float32),
        in_specs=[HBM] + [VMEM] * 6,
        out_specs=HBM,
        scratch_shapes=[
            pltpu.VMEM((held, rows, BW), jnp.float32),
            pltpu.VMEM((len(BANDS), 2 * pairs, BW), jnp.float32),
            pltpu.VMEM((2, len(FACTORS), 2 * pairs, BW), jnp.float32),
            pltpu.SMEM(plan.shape, plan.dtype),
            pltpu.SemaphoreType.DMA((held,)),
            pltpu.SemaphoreType.DMA,
        ],
        compiler_params=PARAMS,
        name="turn_columns",
    )(order, summed, passed, other, mine_shifted, own_half, other_half)


def solution(mesh):
    return jax.shard_map(
        body,
        mesh=mesh,
        in_specs=(P(("groups", "rows"), "pairs"), P()),
        out_specs=P(("groups", "rows"), "pairs"),
        check_vma=False,
    )
```

```python
import functools

import jax
import jax.numpy as jnp
from jax import lax
from jax.experimental import pallas as pl
from jax.experimental.pallas import tpu as pltpu
from jax.sharding import PartitionSpec as P

BW = 128
STEPS = 4
SUB = 8
BANDS = (
    [("uu", d) for d in range(STEPS)]
    + [("ll", d) for d in range(STEPS)]
    + [("ul", d) for d in range(STEPS)]
    + [("lu", d) for d in range(1, STEPS)]
)
SMEM = pl.BlockSpec(memory_space=pltpu.SMEM)
VMEM = pl.BlockSpec(memory_space=pltpu.VMEM)
BAND_ROWS = 16
HBM = pl.BlockSpec(memory_space=pl.ANY)
PARAMS = pltpu.CompilerParams(vmem_limit_bytes=24 * 1024 * 1024)


def ahead(values, d):
    return values if d == 0 else pltpu.roll(values, BW - d, 1)


def columns_of(slot):
    return pl.ds(pl.multiple_of(slot * BW, BW), BW)


def core_of(block, held):
    return lax.div(block, jnp.int32(held))


def slot_of(block, held):
    return lax.rem(block, jnp.int32(held))


def add(total, term):
    return term if total is None else total + term


def parity(row):
    for shift in (8, 4, 2, 1):
        row = row ^ (row >> shift)
    return row & 1


def half_here():
    return lax.axis_index("pairs") ^ parity(lax.axis_index("rows"))


def share_pairs(plan, order, held):
    pairs = plan.shape[1] // 2
    seen = [jnp.int32(0)] * 3
    taken = jnp.int32(0)
    for pair in range(pairs):
        first, second = plan[0, 2 * pair], plan[0, 2 * pair + 1]
        core = core_of(first, held)
        kind = jnp.where(core == core_of(second, held), core, 2)
        count = jnp.where(kind == 2, seen[2], jnp.where(kind == 1, seen[1] + 1, seen[0]))
        half = count & 1
        place = jnp.where(half == 0, taken, pairs // 2 + pair - taken)
        order[0, 2 * place] = first
        order[0, 2 * place + 1] = second
        taken += 1 - half
        seen = [n + jnp.where(kind == k, 1, 0) for k, n in enumerate(seen)]


def shift_kernel(plan, matrix, order, shifted, own, plan_here, order_here, sem, plan_sem, order_sem):
    rows = matrix.shape[0]
    held = matrix.shape[1] // BW

    def fetch(slot):
        columns = columns_of(slot)
        return pltpu.make_async_copy(matrix.at[:, columns], shifted.at[0, :, columns], sem.at[slot])

    for slot in range(held):
        fetch(slot).start()
    plan_copy = pltpu.make_async_copy(plan, plan_here, plan_sem)
    plan_copy.start()

    def one(slot, carry):
        fetch(slot).wait()
        columns = columns_of(slot)
        sums = [None] * STEPS
        for row in range(0, rows, SUB):
            here = shifted[0, pl.ds(row, SUB), columns]
            for d in range(STEPS):
                moved = ahead(here, d)
                sums[d] = add(sums[d], here * moved)
                if d:
                    shifted[d, pl.ds(row, SUB), columns] = moved
        for d in range(STEPS):
            own[slot, d] = sums[d]
        return carry

    lax.fori_loop(0, held // 2, one, 0)
    plan_copy.wait()
    share_pairs(plan_here, order_here, held)
    order_copy = pltpu.make_async_copy(order_here, order, order_sem)
    order_copy.start()
    lax.fori_loop(held // 2, held, one, 0)
    order_copy.wait()


def gram_kernel(order, other, mine_shifted, own, bands, other_shifted, partial):
    rows, width = other.shape
    held = width // BW
    pairs = order.shape[1] // 4
    me = lax.axis_index("pairs")
    base = half_here() * pairs

    def one_pair(pair, carry):
        first, second = order[0, 2 * (base + pair)], order[0, 2 * (base + pair) + 1]
        first_mine, second_mine = core_of(first, held) == me, core_of(second, held) == me

        def go(u_here, l_here):
            def load(here, slot, row):
                at = pl.ds(row, SUB), columns_of(slot)
                if here:
                    return [mine_shifted[(d, *at)] for d in range(STEPS)]
                values = other[at]
                moved = [ahead(values, d) for d in range(STEPS)]
                if u_here or l_here:
                    for d in range(1, STEPS):
                        other_shifted[(d - 1, *at)] = moved[d]
                return moved

            u_slot, l_slot = slot_of(first, held), slot_of(second, held)
            sums = {}
            for row in range(0, rows, SUB):
                u, l = load(u_here, u_slot, row), load(l_here, l_slot, row)
                for kind, d in BANDS:
                    if (kind == "uu" and u_here) or (kind == "ll" and l_here):
                        continue
                    term = (u if kind[0] == "u" else l)[0] * (u if kind[1] == "u" else l)[d]
                    sums[kind, d] = add(sums.get((kind, d)), term)
            for d in range(STEPS):
                if u_here:
                    sums["uu", d] = own[u_slot, d]
                if l_here:
                    sums["ll", d] = own[l_slot, d]
            for n, key in enumerate(BANDS):
                at = pl.multiple_of((n * pairs + pair) * SUB, SUB)
                partial[pl.ds(at, SUB), :] = sums[key]

        for u_here, l_here in ((True, True), (True, False), (False, True), (False, False)):
            pl.when((first_mine == u_here) & (second_mine == l_here))(
                functools.partial(go, u_here, l_here)
            )
        return carry

    lax.fori_loop(0, pairs, one_pair, 0)
    used = len(BANDS) * pairs
    partial[pl.ds(used * SUB, (BAND_ROWS * pairs - used) * SUB), :] = jnp.zeros(
        ((BAND_ROWS * pairs - used) * SUB, BW), jnp.float32
    )
    for row in range(0, BAND_ROWS * pairs, SUB):
        total = None
        for sub in range(SUB):
            total = add(total, partial[pl.ds(row * SUB + sub, SUB, stride=SUB), :])
        bands[pl.ds(row, SUB), :] = total


def shift_rest_kernel(order, bands, other, kept, other_shifted):
    held = other.shape[1] // BW
    pairs = order.shape[1] // 4
    me = lax.axis_index("pairs")
    base = 2 * (1 - half_here()) * pairs
    kept[...] = bands[...]

    def one(i, carry):
        block = order[0, base + i]
        partner = order[0, base + i + 1 - 2 * (i & 1)]

        @pl.when((core_of(block, held) != me) & (core_of(partner, held) == me))
        def _():
            columns = columns_of(slot_of(block, held))
            for row in range(0, other.shape[0], SUB):
                here = other[pl.ds(row, SUB), columns]
                for d in range(1, STEPS):
                    other_shifted[d - 1, pl.ds(row, SUB), columns] = ahead(here, d)

        return carry

    lax.fori_loop(0, 2 * pairs, one, 0)


def rotation(upper, lower, cross):
    spread = lower - upper
    twice = jnp.where(spread >= 0, 2.0 * cross, -2.0 * cross)
    spread = jnp.abs(spread)
    scale = jnp.maximum(spread, jnp.abs(twice))
    zero = scale == 0
    scale = jnp.where(zero, 1.0, scale)
    x = jnp.where(zero, 1.0, spread / scale)
    y = twice / scale
    length = jnp.sqrt(x * x + y * y)
    cos_v = jnp.sqrt(0.5 + 0.5 * (x / length))
    sin_v = y / (2.0 * length * cos_v)
    return cos_v, sin_v


def jacobi_bands(g):
    turns = []
    for step in range(STEPS):
        cos_v, sin_v = rotation(g["uu", 0], g["ll", 0], g["ul", 0])
        turns.append((cos_v, sin_v))
        left = STEPS - 1 - step
        if left == 0:
            break
        new = {}
        for d in range(left + 1):
            cos_d, sin_d = ahead(cos_v, d), ahead(sin_v, d)
            uu, ll, ul = g["uu", d], g["ll", d], g["ul", d]
            lu = g["lu", d] if d else ul
            a, b = cos_v * uu - sin_v * lu, cos_v * ul - sin_v * ll
            e, f = sin_v * uu + cos_v * lu, sin_v * ul + cos_v * ll
            new["uu", d] = cos_d * a - sin_d * b
            new["ul", d] = sin_d * a + cos_d * b
            new["lu", d] = cos_d * e - sin_d * f
            new["ll", d] = sin_d * e + cos_d * f
        g = {}
        for d in range(left):
            g["uu", d] = new["uu", d]
            g["ll", d] = ahead(new["ll", d], 1)
            g["ul", d] = new["ul", d + 1]
            if d:
                g["lu", d] = ahead(new["ul", 0] if d == 1 else new["lu", d - 1], 1)
    return turns


def basis_bands(turns):
    x, y = {("u", 0): 1.0}, {("l", 0): 1.0}
    for step, (cos_v, sin_v) in enumerate(turns):
        if step:
            y = {(kind, i + 1): ahead(value, 1) for (kind, i), value in y.items()}
        keys = sorted(set(x) | set(y))
        new_x, new_y = {}, {}
        for key in keys:
            if key not in y:
                new_x[key], new_y[key] = cos_v * x[key], sin_v * x[key]
            elif key not in x:
                new_x[key], new_y[key] = -sin_v * y[key], cos_v * y[key]
            else:
                new_x[key] = cos_v * x[key] - sin_v * y[key]
                new_y[key] = sin_v * x[key] + cos_v * y[key]
        x, y = new_x, new_y
    return x, y


FACTORS = [(kind, i) for kind in "ul" for i in range(STEPS)]


def turn_kernel(
    order_there,
    summed,
    passed,
    other,
    mine_shifted,
    own_half,
    other_half,
    out,
    turned,
    bands,
    factors,
    order,
    sem,
    order_sem,
):
    rows, width = other.shape
    held = width // BW
    pairs = order.shape[1] // 4
    me = lax.axis_index("pairs")
    half = half_here()
    order_copy = pltpu.make_async_copy(order_there, order, order_sem)
    order_copy.start()
    for n in range(len(BANDS)):
        mine, theirs = summed[pl.ds(n * pairs, pairs), :], passed[pl.ds(n * pairs, pairs), :]
        bands[n, pl.ds(0, pairs), :] = jnp.where(half == 0, mine, theirs)
        bands[n, pl.ds(pairs, pairs), :] = jnp.where(half == 0, theirs, mine)
    x, y = basis_bands(jacobi_bands({key: bands[n] for n, key in enumerate(BANDS)}))
    for n, key in enumerate(FACTORS):
        factors[0, n] = x[key]
        factors[1, n] = y[key]
    order_copy.wait()

    def send(slot):
        return pltpu.make_async_copy(turned.at[slot], out.at[:, columns_of(slot)], sem.at[slot])

    def one_pair(other_shifted, cases, base, i, carry):
        pair = base + i
        first, second = order[0, 2 * pair], order[0, 2 * pair + 1]
        first_mine, second_mine = core_of(first, held) == me, core_of(second, held) == me

        def go(u_here, l_here):
            slots = {"u": slot_of(first, held), "l": slot_of(second, held)}
            here = {"u": u_here, "l": l_here}
            scale = [
                [jnp.broadcast_to(factors[side, n, pl.ds(pair, 1), :], (SUB, BW)) for n in range(len(FACTORS))]
                for side in range(2)
            ]
            for row in range(0, rows, SUB):
                total = [None, None]
                for n, (kind, i) in enumerate(FACTORS):
                    at = pl.ds(row, SUB), columns_of(slots[kind])
                    if here[kind]:
                        value = mine_shifted[(i, *at)]
                    else:
                        value = other_shifted[(i - 1, *at)] if i else other[at]
                    for side, kept in enumerate((u_here, l_here)):
                        if kept:
                            total[side] = add(total[side], scale[side][n] * value)
                if u_here:
                    turned[slots["u"], pl.ds(row, SUB), :] = total[0]
                if l_here:
                    turned[slots["l"], pl.ds(row, SUB), :] = ahead(total[1], BW - (STEPS - 1))
            for kind in "ul":
                if here[kind]:
                    send(slots[kind]).start()

        for u_here, l_here in cases:
            pl.when((first_mine == u_here) & (second_mine == l_here))(
                functools.partial(go, u_here, l_here)
            )
        return carry

    inside, straddling = ((True, True),), ((True, False), (False, True))
    lax.fori_loop(0, 2 * pairs, functools.partial(one_pair, None, inside, 0), 0)
    lax.fori_loop(0, pairs, functools.partial(one_pair, own_half, straddling, half * pairs), 0)
    lax.fori_loop(0, pairs, functools.partial(one_pair, other_half, straddling, (1 - half) * pairs), 0)
    for slot in range(held):
        send(slot).wait()


def exchange(values, step):
    size, cores = lax.axis_size("rows"), lax.axis_size("pairs")
    route = [
        (row * cores + core, (row ^ step) * cores + (core ^ parity(step)))
        for row in range(size)
        for core in range(cores)
    ]
    return lax.ppermute(values, ("rows", "pairs"), route)


def sum_over_rows(values, later):
    size = lax.axis_size("rows")
    if size & (size - 1):
        raise ValueError("rows")
    got = [exchange(values, step) for step in (1, 2, 3) if step < size]
    summed = later
    if got:
        summed = summed + got[0]
    if got[1:]:
        summed = summed + (got[1] + got[2])
    stride = 4
    while stride < size:
        summed = summed + exchange(summed, stride)
        stride *= 2
    return summed


def body(matrix, plan):
    rows, width = matrix.shape
    held = width // BW
    pairs = held // 2
    swap = [(0, 1), (1, 0)]
    other = lax.ppermute(matrix, "pairs", swap)
    cost = pl.CostEstimate(flops=30 * rows * width, bytes_accessed=8 * rows * width, transcendentals=0)
    columns = jax.ShapeDtypeStruct((STEPS - 1, rows, width), jnp.float32)
    bands_shape = jax.ShapeDtypeStruct((BAND_ROWS * pairs, BW), jnp.float32)
    order, mine_shifted, own = pl.pallas_call(
        shift_kernel,
        out_shape=[
            jax.ShapeDtypeStruct(plan.shape, plan.dtype),
            jax.ShapeDtypeStruct((STEPS, rows, width), jnp.float32),
            jax.ShapeDtypeStruct((held, STEPS, SUB, BW), jnp.float32),
        ],
        in_specs=[HBM, HBM],
        out_specs=[HBM, VMEM, VMEM],
        scratch_shapes=[
            pltpu.SMEM(plan.shape, plan.dtype),
            pltpu.SMEM(plan.shape, plan.dtype),
            pltpu.SemaphoreType.DMA((held,)),
            pltpu.SemaphoreType.DMA,
            pltpu.SemaphoreType.DMA,
        ],
        compiler_params=PARAMS,
        cost_estimate=cost,
        name="shift_own",
    )(
        pltpu.with_memory_space_constraint(plan, pltpu.HBM),
        pltpu.with_memory_space_constraint(matrix, pltpu.HBM),
    )
    bands, own_half = pl.pallas_call(
        gram_kernel,
        out_shape=[bands_shape, columns],
        in_specs=[SMEM, VMEM, VMEM, VMEM],
        out_specs=[VMEM, VMEM],
        scratch_shapes=[pltpu.VMEM((BAND_ROWS * pairs * SUB, BW), jnp.float32)],
        compiler_params=PARAMS,
        cost_estimate=cost,
        name="gram_bands",
    )(order, other, mine_shifted, own)
    kept, other_half = pl.pallas_call(
        shift_rest_kernel,
        out_shape=[bands_shape, columns],
        in_specs=[SMEM, VMEM, VMEM],
        out_specs=[VMEM, VMEM],
        compiler_params=PARAMS,
        cost_estimate=cost,
        name="shift_rest",
    )(order, bands, other)
    summed = sum_over_rows(bands, kept)
    passed = lax.ppermute(summed, "pairs", swap)
    return pl.pallas_call(
        turn_kernel,
        out_shape=jax.ShapeDtypeStruct((rows, width), jnp.float32),
        in_specs=[HBM] + [VMEM] * 6,
        out_specs=HBM,
        scratch_shapes=[
            pltpu.VMEM((held, rows, BW), jnp.float32),
            pltpu.VMEM((len(BANDS), 2 * pairs, BW), jnp.float32),
            pltpu.VMEM((2, len(FACTORS), 2 * pairs, BW), jnp.float32),
            pltpu.SMEM(plan.shape, plan.dtype),
            pltpu.SemaphoreType.DMA((held,)),
            pltpu.SemaphoreType.DMA,
        ],
        compiler_params=PARAMS,
        name="turn_columns",
    )(order, summed, passed, other, mine_shifted, own_half, other_half)


def solution(mesh):
    return jax.shard_map(
        body,
        mesh=mesh,
        in_specs=(P(("groups", "rows"), "pairs"), P()),
        out_specs=P(("groups", "rows"), "pairs"),
        check_vma=False,
    )
```

```python
import functools

import jax
import jax.numpy as jnp
from jax import lax
from jax.experimental import pallas as pl
from jax.experimental.pallas import tpu as pltpu
from jax.sharding import PartitionSpec as P

BW = 128
STEPS = 4
SUB = 8
BANDS = (
    [("uu", d) for d in range(STEPS)]
    + [("ll", d) for d in range(STEPS)]
    + [("ul", d) for d in range(STEPS)]
    + [("lu", d) for d in range(1, STEPS)]
)
SMEM = pl.BlockSpec(memory_space=pltpu.SMEM)
VMEM = pl.BlockSpec(memory_space=pltpu.VMEM)
BAND_ROWS = 16
HBM = pl.BlockSpec(memory_space=pl.ANY)
PARAMS = pltpu.CompilerParams(vmem_limit_bytes=24 * 1024 * 1024)


def ahead(values, d):
    return values if d == 0 else pltpu.roll(values, BW - d, 1)


def columns_of(slot):
    return pl.ds(pl.multiple_of(slot * BW, BW), BW)


def core_of(block, held):
    return lax.div(block, jnp.int32(held))


def slot_of(block, held):
    return lax.rem(block, jnp.int32(held))


def add(total, term):
    return term if total is None else total + term


def parity(row):
    row = row & ~2
    for shift in (8, 4, 2, 1):
        row = row ^ (row >> shift)
    return row & 1


def half_here():
    return lax.axis_index("pairs") ^ parity(lax.axis_index("rows"))


def share_pairs(plan, order, held):
    pairs = plan.shape[1] // 2
    seen = [jnp.int32(0)] * 3
    taken = jnp.int32(0)
    for pair in range(pairs):
        first, second = plan[0, 2 * pair], plan[0, 2 * pair + 1]
        core = core_of(first, held)
        kind = jnp.where(core == core_of(second, held), core, 2)
        count = jnp.where(kind == 2, seen[2], jnp.where(kind == 1, seen[1] + 1, seen[0]))
        half = count & 1
        place = jnp.where(half == 0, taken, pairs // 2 + pair - taken)
        order[0, 2 * place] = first
        order[0, 2 * place + 1] = second
        taken += 1 - half
        seen = [n + jnp.where(kind == k, 1, 0) for k, n in enumerate(seen)]


def shift_kernel(plan, matrix, order, shifted, own, plan_here, order_here, sem, plan_sem, order_sem):
    rows = matrix.shape[0]
    held = matrix.shape[1] // BW

    def fetch(slot):
        columns = columns_of(slot)
        return pltpu.make_async_copy(matrix.at[:, columns], shifted.at[0, :, columns], sem.at[slot])

    for slot in range(held):
        fetch(slot).start()
    plan_copy = pltpu.make_async_copy(plan, plan_here, plan_sem)
    plan_copy.start()

    def one(slot, carry):
        fetch(slot).wait()
        columns = columns_of(slot)
        sums = [None] * STEPS
        for row in range(0, rows, SUB):
            here = shifted[0, pl.ds(row, SUB), columns]
            for d in range(STEPS):
                moved = ahead(here, d)
                sums[d] = add(sums[d], here * moved)
                if d:
                    shifted[d, pl.ds(row, SUB), columns] = moved
        for d in range(STEPS):
            own[slot, d] = sums[d]
        return carry

    lax.fori_loop(0, held // 2, one, 0)
    plan_copy.wait()
    share_pairs(plan_here, order_here, held)
    order_copy = pltpu.make_async_copy(order_here, order, order_sem)
    order_copy.start()
    lax.fori_loop(held // 2, held, one, 0)
    order_copy.wait()


def gram_kernel(order, other, mine_shifted, own, bands, other_shifted, partial):
    rows, width = other.shape
    held = width // BW
    pairs = order.shape[1] // 4
    me = lax.axis_index("pairs")
    base = half_here() * pairs

    def one_pair(pair, carry):
        first, second = order[0, 2 * (base + pair)], order[0, 2 * (base + pair) + 1]
        first_mine, second_mine = core_of(first, held) == me, core_of(second, held) == me

        def go(u_here, l_here):
            def load(here, slot, row):
                at = pl.ds(row, SUB), columns_of(slot)
                if here:
                    return [mine_shifted[(d, *at)] for d in range(STEPS)]
                values = other[at]
                moved = [ahead(values, d) for d in range(STEPS)]
                if u_here or l_here:
                    for d in range(1, STEPS):
                        other_shifted[(d - 1, *at)] = moved[d]
                return moved

            u_slot, l_slot = slot_of(first, held), slot_of(second, held)
            sums = {}
            for row in range(0, rows, SUB):
                u, l = load(u_here, u_slot, row), load(l_here, l_slot, row)
                for kind, d in BANDS:
                    if (kind == "uu" and u_here) or (kind == "ll" and l_here):
                        continue
                    term = (u if kind[0] == "u" else l)[0] * (u if kind[1] == "u" else l)[d]
                    sums[kind, d] = add(sums.get((kind, d)), term)
            for d in range(STEPS):
                if u_here:
                    sums["uu", d] = own[u_slot, d]
                if l_here:
                    sums["ll", d] = own[l_slot, d]
            for n, key in enumerate(BANDS):
                at = pl.multiple_of((n * pairs + pair) * SUB, SUB)
                partial[pl.ds(at, SUB), :] = sums[key]

        for u_here, l_here in ((True, True), (True, False), (False, True), (False, False)):
            pl.when((first_mine == u_here) & (second_mine == l_here))(
                functools.partial(go, u_here, l_here)
            )
        return carry

    lax.fori_loop(0, pairs, one_pair, 0)
    used = len(BANDS) * pairs
    partial[pl.ds(used * SUB, (BAND_ROWS * pairs - used) * SUB), :] = jnp.zeros(
        ((BAND_ROWS * pairs - used) * SUB, BW), jnp.float32
    )
    for row in range(0, BAND_ROWS * pairs, SUB):
        total = None
        for sub in range(SUB):
            total = add(total, partial[pl.ds(row * SUB + sub, SUB, stride=SUB), :])
        bands[pl.ds(row, SUB), :] = total


def shift_rest_kernel(order, bands, other, kept, other_shifted):
    held = other.shape[1] // BW
    pairs = order.shape[1] // 4
    me = lax.axis_index("pairs")
    base = 2 * (1 - half_here()) * pairs
    kept[...] = bands[...]

    def one(i, carry):
        block = order[0, base + i]
        partner = order[0, base + i + 1 - 2 * (i & 1)]

        @pl.when((core_of(block, held) != me) & (core_of(partner, held) == me))
        def _():
            columns = columns_of(slot_of(block, held))
            for row in range(0, other.shape[0], SUB):
                here = other[pl.ds(row, SUB), columns]
                for d in range(1, STEPS):
                    other_shifted[d - 1, pl.ds(row, SUB), columns] = ahead(here, d)

        return carry

    lax.fori_loop(0, 2 * pairs, one, 0)


def rotation(upper, lower, cross):
    spread = lower - upper
    twice = jnp.where(spread >= 0, 2.0 * cross, -2.0 * cross)
    spread = jnp.abs(spread)
    scale = jnp.maximum(spread, jnp.abs(twice))
    zero = scale == 0
    scale = jnp.where(zero, 1.0, scale)
    x = jnp.where(zero, 1.0, spread / scale)
    y = twice / scale
    length = jnp.sqrt(x * x + y * y)
    cos_v = jnp.sqrt(0.5 + 0.5 * (x / length))
    sin_v = y / (2.0 * length * cos_v)
    return cos_v, sin_v


def jacobi_bands(g):
    turns = []
    for step in range(STEPS):
        cos_v, sin_v = rotation(g["uu", 0], g["ll", 0], g["ul", 0])
        turns.append((cos_v, sin_v))
        left = STEPS - 1 - step
        if left == 0:
            break
        new = {}
        for d in range(left + 1):
            cos_d, sin_d = ahead(cos_v, d), ahead(sin_v, d)
            uu, ll, ul = g["uu", d], g["ll", d], g["ul", d]
            lu = g["lu", d] if d else ul
            a, b = cos_v * uu - sin_v * lu, cos_v * ul - sin_v * ll
            e, f = sin_v * uu + cos_v * lu, sin_v * ul + cos_v * ll
            new["uu", d] = cos_d * a - sin_d * b
            new["ul", d] = sin_d * a + cos_d * b
            new["lu", d] = cos_d * e - sin_d * f
            new["ll", d] = sin_d * e + cos_d * f
        g = {}
        for d in range(left):
            g["uu", d] = new["uu", d]
            g["ll", d] = ahead(new["ll", d], 1)
            g["ul", d] = new["ul", d + 1]
            if d:
                g["lu", d] = ahead(new["ul", 0] if d == 1 else new["lu", d - 1], 1)
    return turns


def basis_bands(turns):
    x, y = {("u", 0): 1.0}, {("l", 0): 1.0}
    for step, (cos_v, sin_v) in enumerate(turns):
        if step:
            y = {(kind, i + 1): ahead(value, 1) for (kind, i), value in y.items()}
        keys = sorted(set(x) | set(y))
        new_x, new_y = {}, {}
        for key in keys:
            if key not in y:
                new_x[key], new_y[key] = cos_v * x[key], sin_v * x[key]
            elif key not in x:
                new_x[key], new_y[key] = -sin_v * y[key], cos_v * y[key]
            else:
                new_x[key] = cos_v * x[key] - sin_v * y[key]
                new_y[key] = sin_v * x[key] + cos_v * y[key]
        x, y = new_x, new_y
    return x, y


FACTORS = [(kind, i) for kind in "ul" for i in range(STEPS)]


def turn_kernel(
    order_there,
    summed,
    passed,
    other,
    mine_shifted,
    own_half,
    other_half,
    out,
    turned,
    bands,
    factors,
    order,
    sem,
    order_sem,
):
    rows, width = other.shape
    held = width // BW
    pairs = order.shape[1] // 4
    me = lax.axis_index("pairs")
    half = half_here()
    order_copy = pltpu.make_async_copy(order_there, order, order_sem)
    order_copy.start()
    for n in range(len(BANDS)):
        mine, theirs = summed[pl.ds(n * pairs, pairs), :], passed[pl.ds(n * pairs, pairs), :]
        bands[n, pl.ds(0, pairs), :] = jnp.where(half == 0, mine, theirs)
        bands[n, pl.ds(pairs, pairs), :] = jnp.where(half == 0, theirs, mine)
    x, y = basis_bands(jacobi_bands({key: bands[n] for n, key in enumerate(BANDS)}))
    for n, key in enumerate(FACTORS):
        factors[0, n] = x[key]
        factors[1, n] = y[key]
    order_copy.wait()

    def send(slot):
        return pltpu.make_async_copy(turned.at[slot], out.at[:, columns_of(slot)], sem.at[slot])

    def one_pair(other_shifted, cases, base, i, carry):
        pair = base + i
        first, second = order[0, 2 * pair], order[0, 2 * pair + 1]
        first_mine, second_mine = core_of(first, held) == me, core_of(second, held) == me

        def go(u_here, l_here):
            slots = {"u": slot_of(first, held), "l": slot_of(second, held)}
            here = {"u": u_here, "l": l_here}
            scale = [
                [jnp.broadcast_to(factors[side, n, pl.ds(pair, 1), :], (SUB, BW)) for n in range(len(FACTORS))]
                for side in range(2)
            ]
            for row in range(0, rows, SUB):
                total = [None, None]
                for n, (kind, i) in enumerate(FACTORS):
                    at = pl.ds(row, SUB), columns_of(slots[kind])
                    if here[kind]:
                        value = mine_shifted[(i, *at)]
                    else:
                        value = other_shifted[(i - 1, *at)] if i else other[at]
                    for side, kept in enumerate((u_here, l_here)):
                        if kept:
                            total[side] = add(total[side], scale[side][n] * value)
                if u_here:
                    turned[slots["u"], pl.ds(row, SUB), :] = total[0]
                if l_here:
                    turned[slots["l"], pl.ds(row, SUB), :] = ahead(total[1], BW - (STEPS - 1))
            for kind in "ul":
                if here[kind]:
                    send(slots[kind]).start()

        for u_here, l_here in cases:
            pl.when((first_mine == u_here) & (second_mine == l_here))(
                functools.partial(go, u_here, l_here)
            )
        return carry

    inside, straddling = ((True, True),), ((True, False), (False, True))
    lax.fori_loop(0, 2 * pairs, functools.partial(one_pair, None, inside, 0), 0)
    lax.fori_loop(0, pairs, functools.partial(one_pair, own_half, straddling, half * pairs), 0)
    lax.fori_loop(0, pairs, functools.partial(one_pair, other_half, straddling, (1 - half) * pairs), 0)
    for slot in range(held):
        send(slot).wait()


def exchange(values, step):
    size, cores = lax.axis_size("rows"), lax.axis_size("pairs")
    route = [
        (row * cores + core, (row ^ step) * cores + (core ^ parity(step)))
        for row in range(size)
        for core in range(cores)
    ]
    return lax.ppermute(values, ("rows", "pairs"), route)


def sum_over_rows(values, later):
    size = lax.axis_size("rows")
    if size & (size - 1):
        raise ValueError("rows")
    got = [exchange(values, step) for step in (1, 2, 3) if step < size]
    summed = later
    if got:
        summed = summed + got[0]
    if got[1:]:
        summed = summed + (got[1] + got[2])
    stride = 4
    while stride < size:
        summed = summed + exchange(summed, stride)
        stride *= 2
    return summed


def body(matrix, plan):
    rows, width = matrix.shape
    held = width // BW
    pairs = held // 2
    swap = [(0, 1), (1, 0)]
    other = lax.ppermute(matrix, "pairs", swap)
    cost = pl.CostEstimate(flops=30 * rows * width, bytes_accessed=8 * rows * width, transcendentals=0)
    columns = jax.ShapeDtypeStruct((STEPS - 1, rows, width), jnp.float32)
    bands_shape = jax.ShapeDtypeStruct((BAND_ROWS * pairs, BW), jnp.float32)
    order, mine_shifted, own = pl.pallas_call(
        shift_kernel,
        out_shape=[
            jax.ShapeDtypeStruct(plan.shape, plan.dtype),
            jax.ShapeDtypeStruct((STEPS, rows, width), jnp.float32),
            jax.ShapeDtypeStruct((held, STEPS, SUB, BW), jnp.float32),
        ],
        in_specs=[HBM, HBM],
        out_specs=[HBM, VMEM, VMEM],
        scratch_shapes=[
            pltpu.SMEM(plan.shape, plan.dtype),
            pltpu.SMEM(plan.shape, plan.dtype),
            pltpu.SemaphoreType.DMA((held,)),
            pltpu.SemaphoreType.DMA,
            pltpu.SemaphoreType.DMA,
        ],
        compiler_params=PARAMS,
        cost_estimate=cost,
        name="shift_own",
    )(
        pltpu.with_memory_space_constraint(plan, pltpu.HBM),
        pltpu.with_memory_space_constraint(matrix, pltpu.HBM),
    )
    bands, own_half = pl.pallas_call(
        gram_kernel,
        out_shape=[bands_shape, columns],
        in_specs=[SMEM, VMEM, VMEM, VMEM],
        out_specs=[VMEM, VMEM],
        scratch_shapes=[pltpu.VMEM((BAND_ROWS * pairs * SUB, BW), jnp.float32)],
        compiler_params=PARAMS,
        cost_estimate=cost,
        name="gram_bands",
    )(order, other, mine_shifted, own)
    kept, other_half = pl.pallas_call(
        shift_rest_kernel,
        out_shape=[bands_shape, columns],
        in_specs=[SMEM, VMEM, VMEM],
        out_specs=[VMEM, VMEM],
        compiler_params=PARAMS,
        cost_estimate=cost,
        name="shift_rest",
    )(order, bands, other)
    summed = sum_over_rows(bands, kept)
    passed = lax.ppermute(summed, "pairs", swap)
    return pl.pallas_call(
        turn_kernel,
        out_shape=jax.ShapeDtypeStruct((rows, width), jnp.float32),
        in_specs=[HBM] + [VMEM] * 6,
        out_specs=HBM,
        scratch_shapes=[
            pltpu.VMEM((held, rows, BW), jnp.float32),
            pltpu.VMEM((len(BANDS), 2 * pairs, BW), jnp.float32),
            pltpu.VMEM((2, len(FACTORS), 2 * pairs, BW), jnp.float32),
            pltpu.SMEM(plan.shape, plan.dtype),
            pltpu.SemaphoreType.DMA((held,)),
            pltpu.SemaphoreType.DMA,
        ],
        compiler_params=PARAMS,
        name="turn_columns",
    )(order, summed, passed, other, mine_shifted, own_half, other_half)


def solution(mesh):
    return jax.shard_map(
        body,
        mesh=mesh,
        in_specs=(P(("groups", "rows"), "pairs"), P()),
        out_specs=P(("groups", "rows"), "pairs"),
        check_vma=False,
    )
```
